32 devices in a mesh: sub: 8 (over z, x), crow: 4 (over y, core).
Axes of the slice: x: 2, y: 2, z: 4, core: 2. Of those that a mesh axis runs over, the one named last changes fastest.
Arguments:
- deflation: bfloat16 [8, 12288, 128], P('sub', 'crow'), as said below
- diag_op: bfloat16 [8, 96, 128, 128], P('sub', 'crow'), as said below
- upper_op: bfloat16 [8, 96, 128, 128], P('sub', 'crow'), may hold values from -0.022094727 to 0.022094727
- tile_blocks: int32 [8, 4, 16], P('sub', 'crow'), may hold values from 0 to 23
- pair_counts: int32 [8, 8], P('sub'), may hold values from 0 to 8, as said below
- pivot_owner: int32 [8], P('sub'), may hold values from 0 to 3
Outputs:
- schur_self: float32 [1024, 128], P(('sub', 'crow'))
- schur_coupling: float32 [1024, 1024], P(('sub', 'crow'))
- panel: float32 [1024, 32], P(('sub', 'crow'))
The draws below stay inside these ranges and needn't reach their ends.
Inputs may be any that keep to these rules, and one draw needn't show every extreme that they name: deflation has independent columns of different scales. Each diag_op block is symmetric with a positive diagonal, and every A_s is symmetric positive definite. pair_counts[s, j] equals pair_counts[s + o[j], 7 - j], is 0 where s + o[j] lies outside 0 to 7, and the pair of subdomains 0 and 1 shares 8 tiles.
All inputs are finite; a program needn't handle non-finite values.
Results may differ from the reference program's by a relative error of at most 0.0029.
Values may be sent and summed in bfloat16 or wider, within the bound.
A program may use at most 64 MiB of HBM per device.

```python
import math
import jax
import jax.numpy as jnp
from jax import lax

K = 128
TB = 128
RB_DEV = 24
TPD = 2
NB = 8
SUBS = 8
GX = 4
RBS = 96
ROWS = 12288
MAXT = 8
N_CROW = 4


coupling_bound = 0.0221


def draw_deflation(key, part):
    first_key, second_key = jax.random.split(key, 2)
    column_scale = jnp.exp(jax.random.uniform(second_key, (K,), jnp.float32, math.log(0.5), math.log(2.0)))
    values = jnp.clip(jax.random.normal(first_key, (SUBS, ROWS, K), jnp.float32), -6.0, 6.0) * column_scale
    return (values / math.sqrt(TB)).astype(jnp.bfloat16)


def draw_diag_op(key, part):
    first_key, second_key = jax.random.split(key)
    noise = jax.random.uniform(first_key, (SUBS, RBS, TB, TB), jnp.float32, -coupling_bound, coupling_bound)
    symmetric = (noise + jnp.swapaxes(noise, 2, 3)) * 0.7071
    top_value = 4.0
    diagonal = jnp.exp(jax.random.uniform(second_key, (SUBS, RBS, TB), jnp.float32, 0.0, math.log(top_value)))
    return (symmetric + diagonal[..., None] * jnp.eye(TB, dtype=jnp.float32)).astype(jnp.bfloat16)


def draw_pair_counts(key, part):
    first_key, second_key = jax.random.split(jax.random.fold_in(key, 7))
    base_load = jax.random.randint(first_key, (SUBS, SUBS), 0, MAXT // 2 + 1)
    heavy = (jax.random.randint(second_key, (SUBS,), 0, 4) == 0).astype(jnp.int32)
    indices = jnp.arange(SUBS, dtype=jnp.int32)
    lower_index = jnp.minimum(indices[:, None], indices[None, :])
    upper_index = jnp.maximum(indices[:, None], indices[None, :])
    symmetric = base_load[lower_index, upper_index]
    pair_load = jnp.minimum(MAXT, symmetric + 6 * (heavy[:, None] + heavy[None, :]))
    pair_load = pair_load.at[0, 1].set(MAXT).at[1, 0].set(MAXT)
    offsets = [-GX - 1, -GX, -GX + 1, -1, 1, GX - 1, GX, GX + 1]
    columns = []
    for offset_value in offsets:
        target = indices + offset_value
        inside = (target >= 0) & (target < SUBS)
        clipped = jnp.clip(target, 0, SUBS - 1)
        columns.append(jnp.where(inside, pair_load[indices, clipped], 0))
    return jnp.stack(columns, 1).astype(jnp.int32)


def set_ends(values, key, smallest, high):
    longest = values.shape.index(max(values.shape))
    spots = []
    for shift in (0, 1):
        where = [jax.random.randint(jax.random.fold_in(key, axis), (), 0, length) for axis, length in enumerate(values.shape)]
        where[longest] = (where[longest] + shift) % values.shape[longest]
        spots.append(tuple(where))
    return values.at[spots[0]].set(smallest).at[spots[1]].set(high)


def block_levels(key, extent, cuts, low, high):
    gain = 1.0
    for position, shards_of in cuts:
        draws = jax.random.uniform(jax.random.fold_in(jax.random.fold_in(key, 6), position), (shards_of,), jnp.float32, low / len(cuts), high / len(cuts))
        gain = gain * jnp.repeat(jnp.exp(draws), extent[position] // shards_of).reshape((-1,) + (1,) * (len(extent) - 1 - position))
    return gain


def setup_inputs(seed: int = 0) -> dict:
    key_of = jax.random.split(jax.random.key(seed), 7)
    deflation = draw_deflation(jax.random.fold_in(key_of[6], 71), 0)
    diag_op = draw_diag_op(jax.random.fold_in(key_of[6], 71), 0)
    upper_op = jnp.clip(jax.random.uniform(key_of[2], (SUBS, RBS, TB, TB), jnp.float32, -0.022094727, 0.022094727) * block_levels(key_of[2], (SUBS, RBS, TB, TB), ((0, 8), (1, 4)), -0.4, 0.0), -0.022094727, 0.022094727).astype(jnp.bfloat16)
    tile_blocks = set_ends(jax.random.randint(key_of[3], (SUBS, N_CROW, NB * TPD), 0, RB_DEV), jax.random.fold_in(key_of[3], 1), 0, RB_DEV - 1).astype(jnp.int32)
    pair_counts = draw_pair_counts(jax.random.fold_in(key_of[6], 71), 0)
    pivot_owner = set_ends(jax.random.randint(key_of[5], (SUBS,), 0, N_CROW), jax.random.fold_in(key_of[5], 1), 0, N_CROW - 1).astype(jnp.int32)
    return dict(deflation=deflation, diag_op=diag_op, upper_op=upper_op, tile_blocks=tile_blocks, pair_counts=pair_counts, pivot_owner=pivot_owner)


def neighbour_offsets(across):
    return [-across - 1, -across, -across + 1, -1, 1, across - 1, across, across + 1]

def reference(deflation, diag_op, upper_op, tile_blocks, pair_counts, pivot_owner):
    sub_total, row_total, coarse_width = deflation.shape
    block_total, tile_rows = (diag_op.shape[1], diag_op.shape[2])
    block_share = block_total // N_CROW
    slot_count = pair_counts.shape[1]
    per_slot = tile_blocks.shape[2] // slot_count
    row_share = coarse_width // N_CROW

    def apply_local(index):
        vectors = deflation[index].astype(jnp.float32).reshape(block_total, tile_rows, coarse_width)
        diagonal = diag_op[index].astype(jnp.float32)
        upper_blocks = upper_op[index].astype(jnp.float32)
        zero_rows = jnp.zeros((1, tile_rows, coarse_width), jnp.float32)
        zero_block = jnp.zeros((1, tile_rows, tile_rows), jnp.float32)
        before = jnp.concatenate([zero_rows, vectors[:-1]], 0)
        after = jnp.concatenate([vectors[1:], zero_rows], 0)
        lower_blocks = jnp.concatenate([zero_block, upper_blocks[:-1]], 0)
        product = jnp.einsum('bij,bjk->bik', diagonal, vectors) + jnp.einsum('bij,bjk->bik', upper_blocks, after) + jnp.einsum('bji,bjk->bik', lower_blocks, before)
        return product.astype(jnp.bfloat16)
    applied = lax.map(apply_local, jnp.arange(sub_total, dtype=jnp.int32))
    offsets = jnp.array(neighbour_offsets(GX), jnp.int32)
    crow_ids = jnp.arange(N_CROW, dtype=jnp.int32)
    unit_ids = jnp.arange(per_slot, dtype=jnp.int32)
    slot_ids = jnp.arange(slot_count, dtype=jnp.int32)
    opposite = (slot_count - 1 - slot_ids).astype(jnp.int32)

    def coarse_row(index):
        vectors = deflation[index].astype(jnp.float32)
        vector_blocks = vectors.reshape(block_total, tile_rows, coarse_width)
        applied_rows = applied[index].astype(jnp.float32).reshape(row_total, coarse_width)
        gram_part = jnp.einsum('nr,nk->rk', vectors, applied_rows)
        own_blocks = tile_blocks[index].reshape(N_CROW, slot_count, per_slot) + crow_ids[:, None, None] * block_share
        target = index + offsets
        clipped = jnp.clip(target, 0, sub_total - 1).astype(jnp.int32)
        far_lists = tile_blocks[clipped].reshape(slot_count, N_CROW, slot_count, per_slot)
        far_pick = far_lists[slot_ids, :, opposite, :]
        far_blocks = jnp.transpose(far_pick, (1, 0, 2)) + crow_ids[:, None, None] * block_share
        live_mask = crow_ids[:, None, None] * per_slot + unit_ids[None, None, :] < pair_counts[index][None, :, None]
        own_tiles = vector_blocks[own_blocks] * live_mask[..., None, None].astype(jnp.float32)
        far_tiles = applied[clipped[None, :, None], far_blocks].astype(jnp.float32)
        coupling = jnp.einsum('cjutr,cjutk->rjk', own_tiles, far_tiles)
        whole = jnp.concatenate([gram_part[:, None, :], coupling], 1).reshape(coarse_width, (slot_count + 1) * coarse_width)
        owner_index = pivot_owner[index]
        leading = lax.dynamic_slice_in_dim(whole, owner_index * row_share, row_share, 0)
        pivot_block = lax.dynamic_slice_in_dim(leading, owner_index * row_share, row_share, 1)
        factor = jnp.linalg.cholesky(pivot_block)
        solved = jax.scipy.linalg.solve_triangular(factor, leading, lower=True)
        columns = lax.dynamic_slice_in_dim(whole, owner_index * row_share, row_share, 1)
        panel_rows = jax.scipy.linalg.solve_triangular(factor, columns.T, lower=True).T
        updated = whole - jnp.dot(panel_rows, solved, precision=lax.Precision.HIGHEST)
        return (updated[:, :coarse_width], updated[:, coarse_width:], panel_rows)
    self_part, coupling_part, panel_part = lax.map(coarse_row, jnp.arange(sub_total, dtype=jnp.int32))
    return (self_part.reshape(sub_total * coarse_width, coarse_width), coupling_part.reshape(sub_total * coarse_width, slot_count * coarse_width), panel_part.reshape(sub_total * coarse_width, row_share))
```

```python
import functools

import jax
import jax.numpy as jnp
from jax import lax
from jax.experimental import pallas as pl
from jax.experimental.pallas import tpu as pltpu
from jax.sharding import PartitionSpec as P

MESH = pl.DeviceIdType.MESH
HIGHEST = lax.Precision.HIGHEST
F32 = jnp.float32
BF16 = jnp.bfloat16


def neighbour_offsets(across):
    return [-across - 1, -across, -across + 1, -1, 1, across - 1, across, across + 1]


def dot(a, b, dims=((1,), (0,)), precision=None):
    return lax.dot_general(a, b, (dims, ((), ())), precision=precision, preferred_element_type=F32)


def lanes_from(x, owner, share, parts):
    width = x.shape[1]
    chosen = jnp.broadcast_to(owner, x.shape)
    out = x
    for part in range(1, parts):
        out = jnp.where(chosen == part, pltpu.roll(x, width - part * share, 1), out)
    return out


def kernel(
    offsets, sub_count, crow_count, early,
    z_hbm, d_hbm, u_hbm, tiles, counts, owners,
    self_out, coupling_out, panel_out,
    zbuf, dbuf, ubuf, outgoing, arrived, own, product, reduced, partial, grams, gram, gram_t,
    load_sem, halo_send, halo_recv, tile_send, tile_recv, gram_send, gram_recv, red_send, red_recv,
):
    s = lax.axis_index("sub")
    c = lax.axis_index("crow")
    blocks = dbuf.shape[0]
    rows = dbuf.shape[1]
    width = zbuf.shape[2]
    slots = len(offsets)
    per_slot = outgoing.shape[1] // rows
    share = width // crow_count
    peers = [lax.rem(c + r, crow_count) for r in range(1, crow_count)]
    inside = [jnp.logical_and(s + o >= 0, s + o < sub_count) for o in offsets]
    order = [k for pair in zip(range(slots), reversed(range(slots))) for k in pair][:slots]

    loads = [
        pltpu.make_async_copy(z_hbm, zbuf.at[pl.ds(1, blocks)], load_sem.at[0]),
        pltpu.make_async_copy(d_hbm, dbuf, load_sem.at[1]),
        pltpu.make_async_copy(u_hbm, ubuf.at[pl.ds(1, blocks)], load_sem.at[2]),
    ]
    for load in loads:
        load.start()

    barrier = pltpu.get_barrier_semaphore()
    for peer in peers:
        pl.semaphore_signal(barrier, inc=1, device_id={"crow": peer}, device_id_type=MESH)
    expected = crow_count - 1
    for j in range(slots):
        @pl.when(inside[j])
        def _():
            pl.semaphore_signal(barrier, inc=1, device_id={"sub": s + offsets[j]}, device_id_type=MESH)
        expected = expected + jnp.where(inside[j], 1, 0)
    pl.semaphore_wait(barrier, expected)

    has_left, has_right = c > 0, c < crow_count - 1

    def halo(k):
        source, target, peer = (
            (z_hbm.at[blocks - 1], zbuf.at[0], c + 1),
            (u_hbm.at[blocks - 1], ubuf.at[0], c + 1),
            (z_hbm.at[0], zbuf.at[blocks + 1], c - 1),
        )[k]
        return pltpu.make_async_remote_copy(
            src_ref=source, dst_ref=target, send_sem=halo_send.at[k], recv_sem=halo_recv.at[k],
            device_id={"crow": peer}, device_id_type=MESH,
        )

    @pl.when(has_right)
    def _():
        halo(0).start()
        halo(1).start()

    @pl.when(has_left)
    def _():
        halo(2).start()

    @pl.when(jnp.logical_not(has_left))
    def _():
        zbuf[0] = jnp.zeros((rows, width), BF16)
        ubuf[0] = jnp.zeros((rows, rows), BF16)

    @pl.when(jnp.logical_not(has_right))
    def _():
        zbuf[blocks + 1] = jnp.zeros((rows, width), BF16)

    for load in loads:
        load.wait()

    def applied(b):
        row = jnp.concatenate([dbuf[b], ubuf[b + 1]], axis=1)
        column = jnp.concatenate([zbuf[b + 1], zbuf[b + 2]], axis=0)
        total = dot(row, column) + dot(ubuf[b], zbuf[b], ((0,), (0,)))
        return total.astype(BF16)

    def add_gram(b, total):
        return total + dot(zbuf[b + 1], applied(b), ((0,), (0,)))

    total = lax.fori_loop(1, 1 + early, add_gram, jnp.zeros((width, width), F32), unroll=2)

    @pl.when(has_left)
    def _():
        halo(0).wait_recv()
        halo(1).wait_recv()

    @pl.when(has_right)
    def _():
        halo(2).wait_recv()

    def tile_copy(j):
        return pltpu.make_async_remote_copy(
            src_ref=outgoing.at[j], dst_ref=arrived.at[slots - 1 - j],
            send_sem=tile_send.at[j], recv_sem=tile_recv.at[slots - 1 - j],
            device_id={"sub": s + offsets[j]}, device_id_type=MESH,
        )

    for j in order:
        @pl.when(inside[j])
        def _():
            for u in range(per_slot):
                outgoing[j, u * rows:(u + 1) * rows] = applied(tiles[0, 0, j * per_slot + u])
            tile_copy(j).start()

    total = add_gram(0, add_gram(blocks - 1, total))
    total = lax.fori_loop(1 + early, blocks - 1, add_gram, total, unroll=2)
    grams[0] = total

    def gram_copy(r):
        return pltpu.make_async_remote_copy(
            src_ref=grams.at[0], dst_ref=grams.at[r],
            send_sem=gram_send.at[r - 1], recv_sem=gram_recv.at[r - 1],
            device_id={"crow": peers[r - 1]}, device_id_type=MESH,
        )

    for r in range(1, crow_count):
        gram_copy(r).start()

    for j in order:
        @pl.when(inside[slots - 1 - j])
        def _():
            i = slots - 1 - j
            for u in range(per_slot):
                tile = zbuf[tiles[0, 0, i * per_slot + u] + 1].astype(F32)
                limit = jnp.broadcast_to(counts[0, i], tile.shape)
                tile = jnp.where(limit > c * per_slot + u, tile, 0.0)
                own[i, :, u * rows:(u + 1) * rows] = tile.T.astype(BF16)

    for r in range(1, crow_count):
        gram_copy(r).wait_recv()
    whole = grams[0]
    for r in range(1, crow_count):
        whole = whole + grams[r]
    gram[...] = whole.reshape(gram.shape)
    gram_t[...] = whole.T.reshape(gram.shape)

    owner = owners[0]
    leading = gram[owner]
    symmetric = 0.5 * (leading + gram_t[owner])
    symmetric = lanes_from(symmetric, owner, share, crow_count)
    row_id = lax.broadcasted_iota(jnp.int32, (share, width), 0)
    lane_id = lax.broadcasted_iota(jnp.int32, (share, width), 1)
    unit = (lane_id - share == row_id).astype(F32)
    state = jnp.where(lane_id < share, symmetric, unit)
    for k in range(share):
        scale = lax.rsqrt(state[k:k + 1, k:k + 1])
        pivot_row = state[k:k + 1, :] * scale
        step = jnp.where(row_id[:, :1] > k, state[:, k:k + 1] * scale, 0.0)
        state = jnp.where(row_id == k, pivot_row, state - step * pivot_row)
    inverse = pltpu.roll(state, width - share, 1)[:, :share]

    columns = lanes_from(whole, owner, share, crow_count)[:, :share]
    panel_all = dot(columns, inverse, ((1,), (1,)), HIGHEST)
    weights = dot(panel_all, inverse, ((1,), (0,)), HIGHEST)
    updated = whole - dot(weights, leading, ((1,), (0,)), HIGHEST)
    gram_t[...] = updated.reshape(gram.shape)
    self_out[...] = gram_t[c]
    gram_t[:, :, :share] = panel_all.reshape(crow_count, share, share)
    panel_out[...] = gram_t[c, :, :share]

    def red_copy(i, r):
        return pltpu.make_async_remote_copy(
            src_ref=reduced.at[i, peers[r]],
            dst_ref=partial.at[i, r],
            send_sem=red_send.at[i, r], recv_sem=red_recv.at[i, r],
            device_id={"crow": peers[r]}, device_id_type=MESH,
        )

    for j in order:
        i = slots - 1 - j

        @pl.when(inside[i])
        def _():
            tile_copy(j).wait_recv()
            here = dot(own[i], arrived[i])
            product[...] = here.reshape(product.shape)
            here = here - dot(weights, product[owner], ((1,), (0,)), HIGHEST)
            reduced[i] = here.reshape(product.shape)
            for r in range(crow_count - 1):
                red_copy(i, r).start()

    for j in order:
        i = slots - 1 - j

        @pl.when(inside[i])
        def _():
            result = reduced[i, c]
            for r in range(crow_count - 1):
                red_copy(i, r).wait_recv()
                result = result + partial[i, r]
            coupling_out[:, i * width:(i + 1) * width] = result

        @pl.when(jnp.logical_not(inside[i]))
        def _():
            coupling_out[:, i * width:(i + 1) * width] = jnp.zeros((share, width), F32)

    @pl.when(has_right)
    def _():
        halo(0).wait_send()
        halo(1).wait_send()

    @pl.when(has_left)
    def _():
        halo(2).wait_send()

    for r in range(1, crow_count):
        gram_copy(r).wait_send()
    for j in range(slots):
        @pl.when(inside[j])
        def _():
            tile_copy(j).wait_send()
            for r in range(crow_count - 1):
                red_copy(j, r).wait_send()


def per_device(deflation, diag_op, upper_op, tile_blocks, pair_counts, pivot_owner):
    crow_count = lax.axis_size("crow")
    sub_count = lax.axis_size("sub")
    offsets = neighbour_offsets(min(16, sub_count // 2))
    blocks, rows = diag_op.shape[1], diag_op.shape[2]
    width = deflation.shape[2]
    slots = pair_counts.shape[1]
    per_slot = tile_blocks.shape[2] // slots
    share = width // crow_count
    others = crow_count - 1
    vmem = pl.BlockSpec(memory_space=pltpu.VMEM)
    smem = pl.BlockSpec(memory_space=pltpu.SMEM)
    hbm = pl.BlockSpec(memory_space=pl.ANY)
    dma = pltpu.SemaphoreType.DMA
    return pl.pallas_call(
        functools.partial(kernel, offsets, sub_count, crow_count, 8),
        out_shape=(
            jax.ShapeDtypeStruct((share, width), F32),
            jax.ShapeDtypeStruct((share, slots * width), F32),
            jax.ShapeDtypeStruct((share, share), F32),
        ),
        in_specs=[hbm, hbm, hbm, smem, smem, smem],
        out_specs=(vmem, vmem, vmem),
        scratch_shapes=[
            pltpu.VMEM((blocks + 2, rows, width), BF16),
            pltpu.VMEM((blocks, rows, rows), BF16),
            pltpu.VMEM((blocks + 1, rows, rows), BF16),
            pltpu.VMEM((slots, per_slot * rows, width), BF16),
            pltpu.VMEM((slots, per_slot * rows, width), BF16),
            pltpu.VMEM((slots, width, per_slot * rows), BF16),
            pltpu.VMEM((crow_count, share, width), F32),
            pltpu.VMEM((slots, crow_count, share, width), F32),
            pltpu.VMEM((slots, others, share, width), F32),
            pltpu.VMEM((crow_count, width, width), F32),
            pltpu.VMEM((crow_count, share, width), F32),
            pltpu.VMEM((crow_count, share, width), F32),
            dma((3,)), dma((3,)), dma((3,)),
            dma((slots,)), dma((slots,)),
            dma((others,)), dma((others,)),
            dma((slots, others)), dma((slots, others)),
        ],
        compiler_params=pltpu.CompilerParams(
            collective_id=0, has_side_effects=True, vmem_limit_bytes=24 * 1024 * 1024
        ),
    )(
        deflation.reshape(blocks, rows, width),
        diag_op.reshape(blocks, rows, rows),
        upper_op.reshape(blocks, rows, rows),
        tile_blocks, pair_counts, pivot_owner,
    )


def solution(mesh):
    placed = (
        P("sub", "crow", None),
        P("sub", "crow", None, None),
        P("sub", "crow", None, None),
        P("sub", "crow", None),
        P("sub", None),
        P("sub"),
    )
    return jax.shard_map(
        per_device,
        mesh=mesh,
        in_specs=placed,
        out_specs=(P(("sub", "crow"), None), P(("sub", "crow"), None), P(("sub", "crow"), None)),
        check_vma=False,
    )
```

```python
import functools

import jax
import jax.numpy as jnp
from jax import lax
from jax.experimental import pallas as pl
from jax.experimental.pallas import tpu as pltpu
from jax.sharding import PartitionSpec as P

MESH = pl.DeviceIdType.MESH
HIGHEST = lax.Precision.HIGHEST
F32 = jnp.float32
BF16 = jnp.bfloat16
VMEM_BYTES = 56 * 1024 * 1024


def neighbour_offsets(across):
    return [-across - 1, -across, -across + 1, -1, 1, across - 1, across, across + 1]


def dot(a, b, dims=((1,), (0,)), precision=None):
    return lax.dot_general(a, b, (dims, ((), ())), precision=precision, preferred_element_type=F32)


def lanes_from(x, owner, share, parts):
    width = x.shape[1]
    chosen = jnp.broadcast_to(owner, x.shape)
    out = x
    for part in range(1, parts):
        out = jnp.where(chosen == part, pltpu.roll(x, width - part * share, 1), out)
    return out


def kernel(
    offsets, sub_count, crow_count,
    z_hbm, d_hbm, u_hbm, tiles, counts, owners,
    self_out, coupling_out, panel_out,
    zbuf, dbuf, ubuf, abuf, outgoing, arrived, own, product, reduced, partial, pivots, square, panels,
    load_sem, halo_send, halo_recv, tile_send, tile_recv, pivot_send, pivot_recv, red_send, red_recv,
):
    s = lax.axis_index("sub")
    c = lax.axis_index("crow")
    blocks = dbuf.shape[0]
    rows = dbuf.shape[1]
    width = zbuf.shape[2]
    slots = len(offsets)
    per_slot = outgoing.shape[1] // rows
    share = width // crow_count
    others = crow_count - 1
    peers = [lax.rem(c + r, crow_count) for r in range(1, crow_count)]
    inside = [jnp.logical_and(s + o >= 0, s + o < sub_count) for o in offsets]
    order = [k for pair in zip(range(slots), reversed(range(slots))) for k in pair][:slots]

    loads = [
        pltpu.make_async_copy(z_hbm, zbuf.at[pl.ds(1, blocks)], load_sem.at[0]),
        pltpu.make_async_copy(d_hbm, dbuf, load_sem.at[1]),
        pltpu.make_async_copy(u_hbm, ubuf.at[pl.ds(1, blocks)], load_sem.at[2]),
    ]
    for load in loads:
        load.start()

    barrier = pltpu.get_barrier_semaphore()
    for peer in peers:
        pl.semaphore_signal(barrier, inc=1, device_id={"crow": peer}, device_id_type=MESH)
    expected = others
    for j in range(slots):
        @pl.when(inside[j])
        def _():
            pl.semaphore_signal(barrier, inc=1, device_id={"sub": s + offsets[j]}, device_id_type=MESH)
        expected = expected + jnp.where(inside[j], 1, 0)
    pl.semaphore_wait(barrier, expected)

    has_left, has_right = c > 0, c < crow_count - 1

    def halo(k):
        source, target, peer = (
            (z_hbm.at[blocks - 1], zbuf.at[0], c + 1),
            (u_hbm.at[blocks - 1], ubuf.at[0], c + 1),
            (z_hbm.at[0], zbuf.at[blocks + 1], c - 1),
        )[k]
        return pltpu.make_async_remote_copy(
            src_ref=source, dst_ref=target, send_sem=halo_send.at[k], recv_sem=halo_recv.at[k],
            device_id={"crow": peer}, device_id_type=MESH,
        )

    @pl.when(has_right)
    def _():
        halo(0).start()
        halo(1).start()

    @pl.when(has_left)
    def _():
        halo(2).start()

    @pl.when(jnp.logical_not(has_left))
    def _():
        zbuf[0] = jnp.zeros((rows, width), BF16)
        ubuf[0] = jnp.zeros((rows, rows), BF16)

    @pl.when(jnp.logical_not(has_right))
    def _():
        zbuf[blocks + 1] = jnp.zeros((rows, width), BF16)

    for load in loads:
        load.wait()

    def apply(b):
        row = jnp.concatenate([dbuf[b], ubuf[b + 1]], axis=1)
        column = jnp.concatenate([zbuf[b + 1], zbuf[b + 2]], axis=0)
        total = dot(row, column) + dot(ubuf[b], zbuf[b], ((0,), (0,)))
        abuf[b] = total.astype(BF16)

    inner = blocks - 2
    chunk = max(n for n in range(1, 12) if inner % n == 0)

    @pl.loop(0, inner // chunk)
    def _(step):
        for k in range(chunk):
            apply(1 + step * chunk + k)

    @pl.when(has_left)
    def _():
        halo(0).wait_recv()
        halo(1).wait_recv()

    @pl.when(has_right)
    def _():
        halo(2).wait_recv()

    apply(0)
    apply(blocks - 1)

    def tile_copy(j):
        return pltpu.make_async_remote_copy(
            src_ref=outgoing.at[j], dst_ref=arrived.at[slots - 1 - j],
            send_sem=tile_send.at[j], recv_sem=tile_recv.at[slots - 1 - j],
            device_id={"sub": s + offsets[j]}, device_id_type=MESH,
        )

    for j in order:
        @pl.when(inside[j])
        def _():
            for u in range(per_slot):
                outgoing[j, u * rows:(u + 1) * rows] = abuf[tiles[0, 0, j * per_slot + u]]
            tile_copy(j).start()

    group = max(n for n in range(1, 9) if blocks % n == 0)
    gram_t = jnp.zeros((width, width), F32)
    for first in range(0, blocks, group):
        left = abuf[first:first + group].reshape(group * rows, width)
        right = zbuf[first + 1:first + 1 + group].reshape(group * rows, width)
        gram_t = gram_t + dot(left, right, ((0,), (0,)))
    square[...] = gram_t.reshape(square.shape)
    owner = owners[0]
    pivots[0] = square[owner]

    def pivot_copy(r):
        return pltpu.make_async_remote_copy(
            src_ref=pivots.at[0], dst_ref=pivots.at[r],
            send_sem=pivot_send.at[r - 1], recv_sem=pivot_recv.at[r - 1],
            device_id={"crow": peers[r - 1]}, device_id_type=MESH,
        )

    for r in range(1, crow_count):
        pivot_copy(r).start()

    gram = gram_t.T
    product[...] = gram.reshape(product.shape)
    gram_pivot = product[owner]
    for j in order:
        i = slots - 1 - j

        @pl.when(inside[i])
        def _():
            for u in range(per_slot):
                tile = zbuf[tiles[0, 0, i * per_slot + u] + 1].astype(F32)
                limit = jnp.broadcast_to(counts[0, i], tile.shape)
                tile = jnp.where(limit > c * per_slot + u, tile, 0.0)
                own[i, :, u * rows:(u + 1) * rows] = tile.T.astype(BF16)

    for r in range(1, crow_count):
        pivot_copy(r).wait_recv()
    columns = pivots[0]
    for r in range(1, crow_count):
        columns = columns + pivots[r]

    turned = lanes_from(columns, owner, share, crow_count)
    state = 0.5 * (turned[:, :share] + turned.T[:share, :])
    row_id = lax.broadcasted_iota(jnp.int32, (share, width), 0)
    for k in range(share):
        factor = jnp.broadcast_to(state[:, k:k + 1], (share, width))
        scale = lax.rsqrt(factor[k:k + 1, :])
        inverse = scale * scale
        panels[k:k + 1, :] = columns[k:k + 1, :] * scale
        pivot_row = state[k:k + 1, :] * inverse[:, :share]
        column_row = columns[k:k + 1, :] * inverse
        state = jnp.where(row_id[:, :share] == k, pivot_row, state - factor[:, :share] * pivot_row)
        columns = jnp.where(row_id == k, column_row, columns - factor * column_row)
    weights = columns.T

    square[:, :, :share] = panels[...].T.reshape(crow_count, share, share)
    panel_out[...] = square[c, :, :share]

    def red_copy(i, r):
        return pltpu.make_async_remote_copy(
            src_ref=reduced.at[i, peers[r]], dst_ref=partial.at[i, r],
            send_sem=red_send.at[i, r], recv_sem=red_recv.at[i, r],
            device_id={"crow": peers[r]}, device_id_type=MESH,
        )

    def scatter(i, part, pivot_rows):
        part = part - dot(weights, pivot_rows, ((1,), (0,)), HIGHEST)
        reduced[i] = part.reshape(product.shape)
        for r in range(others):
            red_copy(i, r).start()

    def gather(i):
        result = reduced[i, c]
        for r in range(others):
            red_copy(i, r).wait_recv()
            result = result + partial[i, r]
        return result

    scatter(slots, gram, gram_pivot)

    for j in order:
        i = slots - 1 - j

        @pl.when(inside[i])
        def _():
            tile_copy(j).wait_recv()
            here = dot(own[i], arrived[i])
            product[...] = here.reshape(product.shape)
            scatter(i, here, product[owner])

    self_out[...] = gather(slots)
    for j in order:
        i = slots - 1 - j

        @pl.when(inside[i])
        def _():
            coupling_out[:, i * width:(i + 1) * width] = gather(i)

        @pl.when(jnp.logical_not(inside[i]))
        def _():
            coupling_out[:, i * width:(i + 1) * width] = jnp.zeros((share, width), F32)

    @pl.when(has_right)
    def _():
        halo(0).wait_send()
        halo(1).wait_send()

    @pl.when(has_left)
    def _():
        halo(2).wait_send()

    for r in range(1, crow_count):
        pivot_copy(r).wait_send()
        red_copy(slots, r - 1).wait_send()
    for j in range(slots):
        @pl.when(inside[j])
        def _():
            tile_copy(j).wait_send()
            for r in range(others):
                red_copy(j, r).wait_send()


def hand_over(a, b, c, a_out, b_out, c_out, sem):
    copies = [
        pltpu.make_async_copy(source, target, sem.at[k])
        for k, (source, target) in enumerate(((b, b_out), (a, a_out), (c, c_out)))
    ]
    for copy in copies:
        copy.start()
    for copy in copies:
        copy.wait()


def per_device(deflation, diag_op, upper_op, tile_blocks, pair_counts, pivot_owner):
    crow_count = lax.axis_size("crow")
    sub_count = lax.axis_size("sub")
    offsets = neighbour_offsets(min(16, sub_count // 2))
    blocks, rows = diag_op.shape[1], diag_op.shape[2]
    width = deflation.shape[2]
    slots = pair_counts.shape[1]
    per_slot = tile_blocks.shape[2] // slots
    share = width // crow_count
    others = crow_count - 1
    vmem = pl.BlockSpec(memory_space=pltpu.VMEM)
    smem = pl.BlockSpec(memory_space=pltpu.SMEM)
    hbm = pl.BlockSpec(memory_space=pltpu.HBM)
    dma = pltpu.SemaphoreType.DMA
    results = pl.pallas_call(
        functools.partial(kernel, offsets, sub_count, crow_count),
        out_shape=(
            jax.ShapeDtypeStruct((share, width), F32),
            jax.ShapeDtypeStruct((share, slots * width), F32),
            jax.ShapeDtypeStruct((share, share), F32),
        ),
        in_specs=[hbm, hbm, hbm, smem, smem, smem],
        out_specs=(vmem, vmem, vmem),
        scratch_shapes=[
            pltpu.VMEM((blocks + 2, rows, width), BF16),
            pltpu.VMEM((blocks, rows, rows), BF16),
            pltpu.VMEM((blocks + 1, rows, rows), BF16),
            pltpu.VMEM((blocks, rows, width), BF16),
            pltpu.VMEM((slots, per_slot * rows, width), BF16),
            pltpu.VMEM((slots, per_slot * rows, width), BF16),
            pltpu.VMEM((slots, width, per_slot * rows), BF16),
            pltpu.VMEM((crow_count, share, width), F32),
            pltpu.VMEM((slots + 1, crow_count, share, width), F32),
            pltpu.VMEM((slots + 1, others, share, width), F32),
            pltpu.VMEM((crow_count, share, width), F32),
            pltpu.VMEM((crow_count, share, width), F32),
            pltpu.VMEM((share, width), F32),
            dma((3,)), dma((3,)), dma((3,)),
            dma((slots,)), dma((slots,)),
            dma((others,)), dma((others,)),
            dma((slots + 1, others)), dma((slots + 1, others)),
        ],
        compiler_params=pltpu.CompilerParams(
            collective_id=0, has_side_effects=True, vmem_limit_bytes=VMEM_BYTES
        ),
    )(
        deflation.reshape(blocks, rows, width),
        diag_op.reshape(blocks, rows, rows),
        upper_op.reshape(blocks, rows, rows),
        tile_blocks, pair_counts, pivot_owner,
    )
    return pl.pallas_call(
        hand_over,
        out_shape=tuple(jax.ShapeDtypeStruct(x.shape, x.dtype) for x in results),
        in_specs=[hbm] * 3,
        out_specs=(hbm,) * 3,
        scratch_shapes=[dma((3,))],
        compiler_params=pltpu.CompilerParams(vmem_limit_bytes=VMEM_BYTES),
    )(*results)


def solution(mesh):
    placed = (
        P("sub", "crow", None),
        P("sub", "crow", None, None),
        P("sub", "crow", None, None),
        P("sub", "crow", None),
        P("sub", None),
        P("sub"),
    )
    return jax.shard_map(
        per_device,
        mesh=mesh,
        in_specs=placed,
        out_specs=(P(("sub", "crow"), None), P(("sub", "crow"), None), P(("sub", "crow"), None)),
        check_vma=False,
    )
```

```python
import functools

import jax
import jax.numpy as jnp
from jax import lax
from jax.experimental import pallas as pl
from jax.experimental.pallas import tpu as pltpu
from jax.sharding import PartitionSpec as P

MESH = pl.DeviceIdType.MESH
HIGHEST = lax.Precision.HIGHEST
F32 = jnp.float32
BF16 = jnp.bfloat16
VMEM_BYTES = 56 * 1024 * 1024
PIVOTS = 4


def neighbour_offsets(across):
    return [-across - 1, -across, -across + 1, -1, 1, across - 1, across, across + 1]


def dot(a, b, dims=((1,), (0,)), precision=None):
    return lax.dot_general(a, b, (dims, ((), ())), precision=precision, preferred_element_type=F32)


def lanes_from(x, owner, share, parts):
    width = x.shape[1]
    chosen = jnp.broadcast_to(owner, x.shape)
    out = x
    for part in range(1, parts):
        out = jnp.where(chosen == part, pltpu.roll(x, width - part * share, 1), out)
    return out


def kernel(
    offsets, sub_count, crow_count,
    z_hbm, d_hbm, u_hbm, tiles, counts, owners,
    self_out, coupling_out, panel_out,
    zbuf, dbuf, ubuf, abuf, outgoing, arrived, own, product, reduced, partial, pivots, square, panels,
    load_sem, halo_send, halo_recv, tile_send, tile_recv, pivot_send, pivot_recv, red_send, red_recv,
):
    s = lax.axis_index("sub")
    c = lax.axis_index("crow")
    blocks = dbuf.shape[0]
    rows = dbuf.shape[1]
    width = zbuf.shape[2]
    slots = len(offsets)
    per_slot = outgoing.shape[1] // rows
    share = width // crow_count
    others = crow_count - 1
    peers = [lax.rem(c + r, crow_count) for r in range(1, crow_count)]
    inside = [jnp.logical_and(s + o >= 0, s + o < sub_count) for o in offsets]
    order = [k for pair in zip(range(slots), reversed(range(slots))) for k in pair][:slots]

    loads = [
        pltpu.make_async_copy(z_hbm, zbuf.at[pl.ds(1, blocks)], load_sem.at[0]),
        pltpu.make_async_copy(d_hbm, dbuf, load_sem.at[1]),
        pltpu.make_async_copy(u_hbm, ubuf.at[pl.ds(1, blocks)], load_sem.at[2]),
    ]
    for load in loads:
        load.start()

    barrier = pltpu.get_barrier_semaphore()
    for peer in peers:
        pl.semaphore_signal(barrier, inc=1, device_id={"crow": peer}, device_id_type=MESH)
    expected = others
    for j in range(slots):
        @pl.when(inside[j])
        def _():
            pl.semaphore_signal(barrier, inc=1, device_id={"sub": s + offsets[j]}, device_id_type=MESH)
        expected = expected + jnp.where(inside[j], 1, 0)
    pl.semaphore_wait(barrier, expected)

    has_left, has_right = c > 0, c < crow_count - 1

    def halo(k):
        source, target, peer = (
            (z_hbm.at[blocks - 1], zbuf.at[0], c + 1),
            (u_hbm.at[blocks - 1], ubuf.at[0], c + 1),
            (z_hbm.at[0], zbuf.at[blocks + 1], c - 1),
        )[k]
        return pltpu.make_async_remote_copy(
            src_ref=source, dst_ref=target, send_sem=halo_send.at[k], recv_sem=halo_recv.at[k],
            device_id={"crow": peer}, device_id_type=MESH,
        )

    @pl.when(has_right)
    def _():
        halo(0).start()
        halo(1).start()

    @pl.when(has_left)
    def _():
        halo(2).start()

    @pl.when(jnp.logical_not(has_left))
    def _():
        zbuf[0] = jnp.zeros((rows, width), BF16)
        ubuf[0] = jnp.zeros((rows, rows), BF16)

    @pl.when(jnp.logical_not(has_right))
    def _():
        zbuf[blocks + 1] = jnp.zeros((rows, width), BF16)

    for load in loads:
        load.wait()

    def apply(b):
        row = jnp.concatenate([dbuf[b], ubuf[b + 1]], axis=1)
        column = jnp.concatenate([zbuf[b + 1], zbuf[b + 2]], axis=0)
        total = dot(row, column) + dot(ubuf[b], zbuf[b], ((0,), (0,)))
        return total.astype(BF16)

    inner = blocks - 2
    chunk = max(n for n in range(1, 12) if inner % n == 0)

    @pl.when(has_left)
    def _():
        halo(0).wait_recv()
        halo(1).wait_recv()

    @pl.when(has_right)
    def _():
        halo(2).wait_recv()

    def tile_copy(j):
        return pltpu.make_async_remote_copy(
            src_ref=outgoing.at[j], dst_ref=arrived.at[slots - 1 - j],
            send_sem=tile_send.at[j], recv_sem=tile_recv.at[slots - 1 - j],
            device_id={"sub": s + offsets[j]}, device_id_type=MESH,
        )

    for j in order:
        @pl.when(inside[j])
        def _():
            for u in range(per_slot):
                outgoing[j, u * rows:(u + 1) * rows] = apply(tiles[0, 0, j * per_slot + u])
            tile_copy(j).start()

    abuf[0] = apply(0)
    abuf[blocks - 1] = apply(blocks - 1)

    @pl.loop(0, inner // chunk)
    def _(step):
        for k in range(chunk):
            b = 1 + step * chunk + k
            abuf[b] = apply(b)

    group = max(n for n in range(1, 9) if blocks % n == 0)
    gram_t = jnp.zeros((width, width), F32)
    for first in range(0, blocks, group):
        left = abuf[first:first + group].reshape(group * rows, width)
        right = zbuf[first + 1:first + 1 + group].reshape(group * rows, width)
        gram_t = gram_t + dot(left, right, ((0,), (0,)))
    square[...] = gram_t.reshape(square.shape)
    owner = owners[0]
    pivots[0] = square[owner]

    def pivot_copy(r):
        return pltpu.make_async_remote_copy(
            src_ref=pivots.at[0], dst_ref=pivots.at[r],
            send_sem=pivot_send.at[r - 1], recv_sem=pivot_recv.at[r - 1],
            device_id={"crow": peers[r - 1]}, device_id_type=MESH,
        )

    for r in range(1, crow_count):
        pivot_copy(r).start()

    gram = gram_t.T
    product[...] = gram.reshape(product.shape)
    gram_pivot = product[owner]
    for j in order:
        i = slots - 1 - j

        @pl.when(inside[i])
        def _():
            for u in range(per_slot):
                tile = zbuf[tiles[0, 0, i * per_slot + u] + 1].astype(F32)
                limit = jnp.broadcast_to(counts[0, i], tile.shape)
                tile = jnp.where(limit > c * per_slot + u, tile, 0.0)
                own[i, :, u * rows:(u + 1) * rows] = tile.T.astype(BF16)

    for r in range(1, crow_count):
        pivot_copy(r).wait_recv()
    columns = pivots[0]
    for r in range(1, crow_count):
        columns = columns + pivots[r]

    turned = lanes_from(columns, owner, share, crow_count)
    state = 0.5 * (turned[:, :share] + turned.T[:share, :])
    row_id = lax.broadcasted_iota(jnp.int32, (share, width), 0)
    for first in range(0, share, PIVOTS):
        ids = range(PIVOTS)
        factors = [
            jnp.broadcast_to(state[:, first + q:first + q + 1], (share, width)) for q in ids
        ]
        small = [[factors[q][first + p:first + p + 1, :] for q in ids] for p in ids]
        left = [state[first + p:first + p + 1, :] for p in ids]
        right = [columns[first + p:first + p + 1, :] for p in ids]
        for q in ids:
            scale = lax.rsqrt(small[q][q])
            inverse = scale * scale
            panels[first + q:first + q + 1, :] = right[q] * scale
            small[q] = [x * inverse for x in small[q]]
            left[q] = left[q] * inverse[:, :share]
            right[q] = right[q] * inverse
            for p in ids:
                if p != q:
                    ratio = small[p][q]
                    small[p] = [x - ratio * y for x, y in zip(small[p], small[q])]
                    left[p] = left[p] - ratio[:, :share] * left[q]
                    right[p] = right[p] - ratio * right[q]
        for q in ids:
            state = state - factors[q][:, :share] * left[q]
            columns = columns - factors[q] * right[q]
        for q in ids:
            state = jnp.where(row_id[:, :share] == first + q, left[q], state)
            columns = jnp.where(row_id == first + q, right[q], columns)
    weights = columns.T

    square[:, :, :share] = panels[...].T.reshape(crow_count, share, share)
    panel_out[...] = square[c, :, :share]

    def red_copy(i, r):
        return pltpu.make_async_remote_copy(
            src_ref=reduced.at[i, peers[r]], dst_ref=partial.at[i, r],
            send_sem=red_send.at[i, r], recv_sem=red_recv.at[i, r],
            device_id={"crow": peers[r]}, device_id_type=MESH,
        )

    def scatter(i, part, pivot_rows):
        part = part - dot(weights, pivot_rows, ((1,), (0,)), HIGHEST)
        reduced[i] = part.reshape(product.shape)
        for r in range(others):
            red_copy(i, r).start()

    def gather(i):
        result = reduced[i, c]
        for r in range(others):
            red_copy(i, r).wait_recv()
            result = result + partial[i, r]
        return result

    scatter(slots, gram, gram_pivot)

    for j in order:
        i = slots - 1 - j

        @pl.when(inside[i])
        def _():
            tile_copy(j).wait_recv()
            here = dot(own[i], arrived[i])
            product[...] = here.reshape(product.shape)
            scatter(i, here, product[owner])

    self_out[...] = gather(slots)
    for j in order:
        i = slots - 1 - j

        @pl.when(inside[i])
        def _():
            coupling_out[:, i * width:(i + 1) * width] = gather(i)

        @pl.when(jnp.logical_not(inside[i]))
        def _():
            coupling_out[:, i * width:(i + 1) * width] = jnp.zeros((share, width), F32)

    @pl.when(has_right)
    def _():
        halo(0).wait_send()
        halo(1).wait_send()

    @pl.when(has_left)
    def _():
        halo(2).wait_send()

    for r in range(1, crow_count):
        pivot_copy(r).wait_send()
        red_copy(slots, r - 1).wait_send()
    for j in range(slots):
        @pl.when(inside[j])
        def _():
            tile_copy(j).wait_send()
            for r in range(others):
                red_copy(j, r).wait_send()


def hand_over(a, b, c, a_out, b_out, c_out):
    a_out[...] = a[...]
    b_out[...] = b[...]
    c_out[...] = c[...]


def per_device(deflation, diag_op, upper_op, tile_blocks, pair_counts, pivot_owner):
    crow_count = lax.axis_size("crow")
    sub_count = lax.axis_size("sub")
    offsets = neighbour_offsets(min(16, sub_count // 2))
    blocks, rows = diag_op.shape[1], diag_op.shape[2]
    width = deflation.shape[2]
    slots = pair_counts.shape[1]
    per_slot = tile_blocks.shape[2] // slots
    share = width // crow_count
    others = crow_count - 1
    vmem = pl.BlockSpec(memory_space=pltpu.VMEM)
    smem = pl.BlockSpec(memory_space=pltpu.SMEM)
    hbm = pl.BlockSpec(memory_space=pltpu.HBM)
    dma = pltpu.SemaphoreType.DMA
    results = pl.pallas_call(
        functools.partial(kernel, offsets, sub_count, crow_count),
        out_shape=(
            pltpu.VMEM((share, width), F32),
            pltpu.VMEM((share, slots * width), F32),
            pltpu.VMEM((share, share), F32),
        ),
        in_specs=[hbm, hbm, hbm, smem, smem, smem],
        out_specs=(vmem, vmem, vmem),
        scratch_shapes=[
            pltpu.VMEM((blocks + 2, rows, width), BF16),
            pltpu.VMEM((blocks, rows, rows), BF16),
            pltpu.VMEM((blocks + 1, rows, rows), BF16),
            pltpu.VMEM((blocks, rows, width), BF16),
            pltpu.VMEM((slots, per_slot * rows, width), BF16),
            pltpu.VMEM((slots, per_slot * rows, width), BF16),
            pltpu.VMEM((slots, width, per_slot * rows), BF16),
            pltpu.VMEM((crow_count, share, width), F32),
            pltpu.VMEM((slots + 1, crow_count, share, width), F32),
            pltpu.VMEM((slots + 1, others, share, width), F32),
            pltpu.VMEM((crow_count, share, width), F32),
            pltpu.VMEM((crow_count, share, width), F32),
            pltpu.VMEM((share, width), F32),
            dma((3,)), dma((3,)), dma((3,)),
            dma((slots,)), dma((slots,)),
            dma((others,)), dma((others,)),
            dma((slots + 1, others)), dma((slots + 1, others)),
        ],
        compiler_params=pltpu.CompilerParams(
            collective_id=0, has_side_effects=True, vmem_limit_bytes=VMEM_BYTES
        ),
    )(
        deflation.reshape(blocks, rows, width),
        diag_op.reshape(blocks, rows, rows),
        upper_op.reshape(blocks, rows, rows),
        tile_blocks, pair_counts, pivot_owner,
    )
    return pl.pallas_call(
        hand_over,
        out_shape=tuple(jax.ShapeDtypeStruct(x.shape, F32) for x in results),
        in_specs=[vmem] * 3,
        out_specs=(vmem,) * 3,
    )(*results)


def solution(mesh):
    placed = (
        P("sub", "crow", None),
        P("sub", "crow", None, None),
        P("sub", "crow", None, None),
        P("sub", "crow", None),
        P("sub", None),
        P("sub"),
    )
    return jax.shard_map(
        per_device,
        mesh=mesh,
        in_specs=placed,
        out_specs=(P(("sub", "crow"), None), P(("sub", "crow"), None), P(("sub", "crow"), None)),
        check_vma=False,
    )
```

```python
import functools

import jax
import jax.numpy as jnp
from jax import lax
from jax.experimental import pallas as pl
from jax.experimental.pallas import tpu as pltpu
from jax.sharding import PartitionSpec as P

MESH = pl.DeviceIdType.MESH
HIGHEST = lax.Precision.HIGHEST
F32 = jnp.float32
BF16 = jnp.bfloat16
VMEM_BYTES = 56 * 1024 * 1024
PIVOTS = 4


def neighbour_offsets(across):
    return [-across - 1, -across, -across + 1, -1, 1, across - 1, across, across + 1]


def dot(a, b, dims=((1,), (0,)), precision=None):
    return lax.dot_general(a, b, (dims, ((), ())), precision=precision, preferred_element_type=F32)


def lanes_from(x, owner, share, parts):
    width = x.shape[1]
    chosen = jnp.broadcast_to(owner, x.shape)
    out = x
    for part in range(1, parts):
        out = jnp.where(chosen == part, pltpu.roll(x, width - part * share, 1), out)
    return out


def kernel(
    offsets, sub_count, crow_count,
    z_hbm, d_hbm, u_hbm, tiles, counts, owners,
    self_out, coupling_out, panel_out,
    zbuf, ztbuf, dbuf, ubuf, abuf, outgoing, arrived, own, product, reduced, partial, pivots, square, panels,
    load_sem, halo_send, halo_recv, tile_send, tile_recv, pivot_send, pivot_recv, red_send, red_recv,
):
    s = lax.axis_index("sub")
    c = lax.axis_index("crow")
    blocks = dbuf.shape[0]
    rows = dbuf.shape[1]
    width = zbuf.shape[2]
    slots = len(offsets)
    per_slot = outgoing.shape[1]
    share = width // crow_count
    others = crow_count - 1
    peers = [lax.rem(c + r, crow_count) for r in range(1, crow_count)]
    inside = [jnp.logical_and(s + o >= 0, s + o < sub_count) for o in offsets]
    order = [k for pair in zip(range(slots), reversed(range(slots))) for k in pair][:slots]

    loads = [
        pltpu.make_async_copy(z_hbm, zbuf.at[pl.ds(1, blocks)], load_sem.at[0]),
        pltpu.make_async_copy(d_hbm, dbuf, load_sem.at[1]),
        pltpu.make_async_copy(u_hbm, ubuf.at[pl.ds(1, blocks)], load_sem.at[2]),
    ]
    for load in loads:
        load.start()

    barrier = pltpu.get_barrier_semaphore()
    for peer in peers:
        pl.semaphore_signal(barrier, inc=1, device_id={"crow": peer}, device_id_type=MESH)
    expected = others
    for j in range(slots):
        @pl.when(inside[j])
        def _():
            pl.semaphore_signal(barrier, inc=1, device_id={"sub": s + offsets[j]}, device_id_type=MESH)
        expected = expected + jnp.where(inside[j], 1, 0)
    pl.semaphore_wait(barrier, expected)

    has_left, has_right = c > 0, c < crow_count - 1

    def halo(k):
        source, target, peer = (
            (z_hbm.at[blocks - 1], zbuf.at[0], c + 1),
            (u_hbm.at[blocks - 1], ubuf.at[0], c + 1),
            (z_hbm.at[0], zbuf.at[blocks + 1], c - 1),
        )[k]
        return pltpu.make_async_remote_copy(
            src_ref=source, dst_ref=target, send_sem=halo_send.at[k], recv_sem=halo_recv.at[k],
            device_id={"crow": peer}, device_id_type=MESH,
        )

    @pl.when(has_right)
    def _():
        halo(0).start()
        halo(1).start()

    @pl.when(has_left)
    def _():
        halo(2).start()

    @pl.when(jnp.logical_not(has_left))
    def _():
        zbuf[0] = jnp.zeros((rows, width), BF16)
        ubuf[0] = jnp.zeros((rows, rows), BF16)

    @pl.when(jnp.logical_not(has_right))
    def _():
        zbuf[blocks + 1] = jnp.zeros((rows, width), BF16)

    for load in loads:
        load.wait()

    unroll = max(n for n in range(1, 13) if blocks % n == 0)

    @pl.loop(0, blocks // unroll)
    def _(step):
        for k in range(unroll):
            b = 1 + step * unroll + k
            ztbuf[b] = zbuf[b].T

    def apply(b):
        row = jnp.concatenate([ztbuf[b], ztbuf[b + 1]], axis=1)
        column = jnp.concatenate([ubuf[b], dbuf[b]], axis=0)
        total = dot(row, column) + dot(ztbuf[b + 2], ubuf[b + 1], ((1,), (1,)))
        return total.astype(BF16)

    @pl.when(has_left)
    def _():
        halo(0).wait_recv()
        halo(1).wait_recv()

    @pl.when(has_right)
    def _():
        halo(2).wait_recv()

    ztbuf[0] = zbuf[0].T
    ztbuf[blocks + 1] = zbuf[blocks + 1].T

    def tile_copy(j):
        return pltpu.make_async_remote_copy(
            src_ref=outgoing.at[j], dst_ref=arrived.at[slots - 1 - j],
            send_sem=tile_send.at[j], recv_sem=tile_recv.at[slots - 1 - j],
            device_id={"sub": s + offsets[j]}, device_id_type=MESH,
        )

    for j in order:
        @pl.when(inside[j])
        def _():
            for u in range(per_slot):
                outgoing[j, u] = apply(tiles[0, 0, j * per_slot + u])
            tile_copy(j).start()

    @pl.loop(0, blocks // unroll)
    def _(step):
        for k in range(unroll):
            b = step * unroll + k
            abuf[b] = apply(b)

    gram_t = jnp.zeros((width, width), F32)
    for first in range(0, blocks, unroll):
        left = jnp.concatenate([abuf[first + k] for k in range(unroll)], axis=1)
        right = zbuf[first + 1:first + 1 + unroll].reshape(unroll * rows, width)
        gram_t = gram_t + dot(left, right)
    square[...] = gram_t.reshape(square.shape)
    owner = owners[0]
    pivots[0] = square[owner]

    def pivot_copy(r):
        return pltpu.make_async_remote_copy(
            src_ref=pivots.at[0], dst_ref=pivots.at[r],
            send_sem=pivot_send.at[r - 1], recv_sem=pivot_recv.at[r - 1],
            device_id={"crow": peers[r - 1]}, device_id_type=MESH,
        )

    for r in range(1, crow_count):
        pivot_copy(r).start()

    gram = gram_t.T
    product[...] = gram.reshape(product.shape)
    gram_pivot = product[owner]
    for j in order:
        i = slots - 1 - j

        @pl.when(inside[i])
        def _():
            for u in range(per_slot):
                tile = ztbuf[tiles[0, 0, i * per_slot + u] + 1].astype(F32)
                limit = jnp.broadcast_to(counts[0, i], tile.shape)
                tile = jnp.where(limit > c * per_slot + u, tile, 0.0)
                own[i, :, u * rows:(u + 1) * rows] = tile.astype(BF16)

    for r in range(1, crow_count):
        pivot_copy(r).wait_recv()
    columns = pivots[0]
    for r in range(1, crow_count):
        columns = columns + pivots[r]

    turned = lanes_from(columns, owner, share, crow_count)
    state = 0.5 * (turned[:, :share] + turned.T[:share, :])
    row_id = lax.broadcasted_iota(jnp.int32, (share, width), 0)
    for first in range(0, share, PIVOTS):
        ids = range(PIVOTS)
        factors = [
            jnp.broadcast_to(state[:, first + q:first + q + 1], (share, width)) for q in ids
        ]
        small = [[factors[q][first + p:first + p + 1, :] for q in ids] for p in ids]
        left = [state[first + p:first + p + 1, :] for p in ids]
        right = [columns[first + p:first + p + 1, :] for p in ids]
        for q in ids:
            scale = lax.rsqrt(small[q][q])
            inverse = scale * scale
            panels[first + q:first + q + 1, :] = right[q] * scale
            small[q] = [x * inverse for x in small[q]]
            left[q] = left[q] * inverse[:, :share]
            right[q] = right[q] * inverse
            for p in ids:
                if p != q:
                    ratio = small[p][q]
                    small[p] = [x - ratio * y for x, y in zip(small[p], small[q])]
                    left[p] = left[p] - ratio[:, :share] * left[q]
                    right[p] = right[p] - ratio * right[q]
        for q in ids:
            state = state - factors[q][:, :share] * left[q]
            columns = columns - factors[q] * right[q]
        for q in ids:
            state = jnp.where(row_id[:, :share] == first + q, left[q], state)
            columns = jnp.where(row_id == first + q, right[q], columns)
    weights = columns.T

    square[:, :, :share] = panels[...].T.reshape(crow_count, share, share)
    panel_out[...] = square[c, :, :share]

    def red_copy(i, r):
        return pltpu.make_async_remote_copy(
            src_ref=reduced.at[i, peers[r]], dst_ref=partial.at[i, r],
            send_sem=red_send.at[i, r], recv_sem=red_recv.at[i, r],
            device_id={"crow": peers[r]}, device_id_type=MESH,
        )

    def scatter(i, part, pivot_rows):
        part = part - dot(weights, pivot_rows, ((1,), (0,)), HIGHEST)
        reduced[i] = part.reshape(product.shape)
        for r in range(others):
            red_copy(i, r).start()

    def gather(i):
        result = reduced[i, c]
        for r in range(others):
            red_copy(i, r).wait_recv()
            result = result + partial[i, r]
        return result

    scatter(slots, gram, gram_pivot)

    for j in order:
        i = slots - 1 - j

        @pl.when(inside[i])
        def _():
            tile_copy(j).wait_recv()
            far = jnp.concatenate([arrived[i, u] for u in range(per_slot)], axis=1)
            here = dot(own[i], far, ((1,), (1,)))
            product[...] = here.reshape(product.shape)
            scatter(i, here, product[owner])

    self_out[...] = gather(slots)
    for j in order:
        i = slots - 1 - j

        @pl.when(inside[i])
        def _():
            coupling_out[:, i * width:(i + 1) * width] = gather(i)

        @pl.when(jnp.logical_not(inside[i]))
        def _():
            coupling_out[:, i * width:(i + 1) * width] = jnp.zeros((share, width), F32)

    @pl.when(has_right)
    def _():
        halo(0).wait_send()
        halo(1).wait_send()

    @pl.when(has_left)
    def _():
        halo(2).wait_send()

    for r in range(1, crow_count):
        pivot_copy(r).wait_send()
        red_copy(slots, r - 1).wait_send()
    for j in range(slots):
        @pl.when(inside[j])
        def _():
            tile_copy(j).wait_send()
            for r in range(others):
                red_copy(j, r).wait_send()


def hand_over(a, b, c, a_out, b_out, c_out, sem):
    copies = [
        pltpu.make_async_copy(source, target, sem.at[k])
        for k, (source, target) in enumerate(((b, b_out), (a, a_out), (c, c_out)))
    ]
    for copy in copies:
        copy.start()
    for copy in copies:
        copy.wait()


def per_device(deflation, diag_op, upper_op, tile_blocks, pair_counts, pivot_owner):
    crow_count = lax.axis_size("crow")
    sub_count = lax.axis_size("sub")
    offsets = neighbour_offsets(min(16, sub_count // 2))
    blocks, rows = diag_op.shape[1], diag_op.shape[2]
    width = deflation.shape[2]
    slots = pair_counts.shape[1]
    per_slot = tile_blocks.shape[2] // slots
    share = width // crow_count
    others = crow_count - 1
    vmem = pl.BlockSpec(memory_space=pltpu.VMEM)
    smem = pl.BlockSpec(memory_space=pltpu.SMEM)
    hbm = pl.BlockSpec(memory_space=pltpu.HBM)
    dma = pltpu.SemaphoreType.DMA
    results = pl.pallas_call(
        functools.partial(kernel, offsets, sub_count, crow_count),
        out_shape=(
            pltpu.VMEM((share, width), F32),
            pltpu.VMEM((share, slots * width), F32),
            pltpu.VMEM((share, share), F32),
        ),
        in_specs=[hbm, hbm, hbm, smem, smem, smem],
        out_specs=(vmem, vmem, vmem),
        scratch_shapes=[
            pltpu.VMEM((blocks + 2, rows, width), BF16),
            pltpu.VMEM((blocks + 2, width, rows), BF16),
            pltpu.VMEM((blocks, rows, rows), BF16),
            pltpu.VMEM((blocks + 1, rows, rows), BF16),
            pltpu.VMEM((blocks, width, rows), BF16),
            pltpu.VMEM((slots, per_slot, width, rows), BF16),
            pltpu.VMEM((slots, per_slot, width, rows), BF16),
            pltpu.VMEM((slots, width, per_slot * rows), BF16),
            pltpu.VMEM((crow_count, share, width), F32),
            pltpu.VMEM((slots + 1, crow_count, share, width), F32),
            pltpu.VMEM((slots + 1, others, share, width), F32),
            pltpu.VMEM((crow_count, share, width), F32),
            pltpu.VMEM((crow_count, share, width), F32),
            pltpu.VMEM((share, width), F32),
            dma((3,)), dma((3,)), dma((3,)),
            dma((slots,)), dma((slots,)),
            dma((others,)), dma((others,)),
            dma((slots + 1, others)), dma((slots + 1, others)),
        ],
        compiler_params=pltpu.CompilerParams(
            collective_id=0, has_side_effects=True, vmem_limit_bytes=VMEM_BYTES
        ),
    )(
        deflation.reshape(blocks, rows, width),
        diag_op.reshape(blocks, rows, rows),
        upper_op.reshape(blocks, rows, rows),
        tile_blocks, pair_counts, pivot_owner,
    )
    return pl.pallas_call(
        hand_over,
        out_shape=tuple(jax.ShapeDtypeStruct(x.shape, F32) for x in results),
        in_specs=[vmem] * 3,
        out_specs=(hbm,) * 3,
        scratch_shapes=[dma((3,))],
        compiler_params=pltpu.CompilerParams(vmem_limit_bytes=2 * 1024 * 1024),
    )(*results)


def solution(mesh):
    placed = (
        P("sub", "crow", None),
        P("sub", "crow", None, None),
        P("sub", "crow", None, None),
        P("sub", "crow", None),
        P("sub", None),
        P("sub"),
    )
    return jax.shard_map(
        per_device,
        mesh=mesh,
        in_specs=placed,
        out_specs=(P(("sub", "crow"), None), P(("sub", "crow"), None), P(("sub", "crow"), None)),
        check_vma=False,
    )
```

```python
import functools

import jax
import jax.numpy as jnp
from jax import lax
from jax.experimental import pallas as pl
from jax.experimental.pallas import tpu as pltpu
from jax.sharding import PartitionSpec as P

MESH = pl.DeviceIdType.MESH
F32 = jnp.float32
BF16 = jnp.bfloat16
VMEM_BYTES = 56 * 1024 * 1024
PIVOTS = 4


def neighbour_offsets(across):
    return [-across - 1, -across, -across + 1, -1, 1, across - 1, across, across + 1]


def dot(a, b, dims=((1,), (0,)), precision=None):
    return lax.dot_general(a, b, (dims, ((), ())), precision=precision, preferred_element_type=F32)


def lanes_from(x, owner, share, parts):
    width = x.shape[1]
    chosen = jnp.broadcast_to(owner, x.shape)
    out = x
    for part in range(1, parts):
        out = jnp.where(chosen == part, pltpu.roll(x, width - part * share, 1), out)
    return out


def thirds(x):
    first = x.astype(BF16)
    rest = x - first.astype(F32)
    second = rest.astype(BF16)
    return first, second, (rest - second.astype(F32)).astype(BF16)


def kernel(
    offsets, sub_count, crow_count,
    z_hbm, d_hbm, u_hbm, tiles, counts, owners,
    self_out, coupling_out, panel_out,
    zbuf, ztbuf, dbuf, ubuf, abuf, outgoing, arrived, own, product, reduced, partial, pivots, square, panels,
    load_sem, halo_send, halo_recv, tile_send, tile_recv, pivot_send, pivot_recv, red_send, red_recv,
):
    s = lax.axis_index("sub")
    c = lax.axis_index("crow")
    blocks = dbuf.shape[0]
    rows = dbuf.shape[1]
    width = zbuf.shape[2]
    slots = len(offsets)
    per_slot = outgoing.shape[1] // rows
    share = width // crow_count
    others = crow_count - 1
    peers = [lax.rem(c + r, crow_count) for r in range(1, crow_count)]
    inside = [jnp.logical_and(s + o >= 0, s + o < sub_count) for o in offsets]
    order = [k for pair in zip(range(slots), reversed(range(slots))) for k in pair][:slots]

    half = (blocks + 1) // 2
    loads = [
        pltpu.make_async_copy(
            source.at[pl.ds(first, count)], target.at[pl.ds(first + pad, count)], load_sem.at[k, h]
        )
        for h, (first, count) in enumerate(((0, half), (half, blocks - half)))
        for k, (source, target, pad) in enumerate(((z_hbm, zbuf, 1), (u_hbm, ubuf, 1), (d_hbm, dbuf, 0)))
    ]
    for load in loads:
        load.start()

    barrier = pltpu.get_barrier_semaphore()
    for peer in peers:
        pl.semaphore_signal(barrier, inc=1, device_id={"crow": peer}, device_id_type=MESH)
    expected = others
    for j in range(slots):
        @pl.when(inside[j])
        def _():
            pl.semaphore_signal(barrier, inc=1, device_id={"sub": s + offsets[j]}, device_id_type=MESH)
        expected = expected + jnp.where(inside[j], 1, 0)
    pl.semaphore_wait(barrier, expected)

    has_left, has_right = c > 0, c < crow_count - 1

    def halo(k):
        source, target, peer = (
            (z_hbm.at[blocks - 1], zbuf.at[0], c + 1),
            (u_hbm.at[blocks - 1], ubuf.at[0], c + 1),
            (z_hbm.at[0], zbuf.at[blocks + 1], c - 1),
        )[k]
        return pltpu.make_async_remote_copy(
            src_ref=source, dst_ref=target, send_sem=halo_send.at[k], recv_sem=halo_recv.at[k],
            device_id={"crow": peer}, device_id_type=MESH,
        )

    @pl.when(has_right)
    def _():
        halo(0).start()
        halo(1).start()

    @pl.when(has_left)
    def _():
        halo(2).start()

    @pl.when(jnp.logical_not(has_left))
    def _():
        zbuf[0] = jnp.zeros((rows, width), BF16)
        ubuf[0] = jnp.zeros((rows, rows), BF16)

    @pl.when(jnp.logical_not(has_right))
    def _():
        zbuf[blocks + 1] = jnp.zeros((rows, width), BF16)

    for load in loads:
        load.wait()

    unroll = max(n for n in range(1, 13) if blocks % n == 0)
    for k in range(unroll):
        ztbuf[1 + k] = zbuf[1 + k].T

    def apply(b):
        row = jnp.concatenate([dbuf[b], ubuf[b + 1]], axis=1)
        column = jnp.concatenate([zbuf[b + 1], zbuf[b + 2]], axis=0)
        total = dot(row, column) + dot(ubuf[b], zbuf[b], ((0,), (0,)))
        return total.astype(BF16)

    def apply_t(b):
        row = jnp.concatenate([ztbuf[b], ztbuf[b + 1]], axis=1)
        column = jnp.concatenate([ubuf[b], dbuf[b]], axis=0)
        total = dot(row, column) + dot(ztbuf[b + 2], ubuf[b + 1], ((1,), (1,)))
        return total.astype(BF16)

    @pl.when(has_left)
    def _():
        halo(0).wait_recv()
        halo(1).wait_recv()

    @pl.when(has_right)
    def _():
        halo(2).wait_recv()

    def tile_copy(j):
        return pltpu.make_async_remote_copy(
            src_ref=outgoing.at[j], dst_ref=arrived.at[slots - 1 - j],
            send_sem=tile_send.at[j], recv_sem=tile_recv.at[slots - 1 - j],
            device_id={"sub": s + offsets[j]}, device_id_type=MESH,
        )

    for j in order:
        @pl.when(inside[j])
        def _():
            for u in range(per_slot):
                outgoing[j, u * rows:(u + 1) * rows] = apply(tiles[0, 0, j * per_slot + u])
            tile_copy(j).start()

    @pl.loop(1, blocks // unroll)
    def _(step):
        for k in range(unroll):
            b = 1 + step * unroll + k
            ztbuf[b] = zbuf[b].T

    ztbuf[0] = zbuf[0].T
    ztbuf[blocks + 1] = zbuf[blocks + 1].T

    @pl.loop(0, blocks // unroll)
    def _(step):
        for k in range(unroll):
            b = step * unroll + k
            abuf[b] = apply_t(b)

    gram_t = jnp.zeros((width, width), F32)
    for first in range(0, blocks, unroll):
        left = jnp.concatenate([abuf[first + k] for k in range(unroll)], axis=1)
        right = zbuf[first + 1:first + 1 + unroll].reshape(unroll * rows, width)
        gram_t = gram_t + dot(left, right)
    square[...] = gram_t.reshape(square.shape)
    owner = owners[0]
    pivots[0] = square[owner]

    def pivot_copy(r):
        return pltpu.make_async_remote_copy(
            src_ref=pivots.at[0], dst_ref=pivots.at[r],
            send_sem=pivot_send.at[r - 1], recv_sem=pivot_recv.at[r - 1],
            device_id={"crow": peers[r - 1]}, device_id_type=MESH,
        )

    for r in range(1, crow_count):
        pivot_copy(r).start()

    gram = gram_t.T
    product[...] = gram.reshape(product.shape)
    gram_pivot = product[owner]
    for j in order:
        i = slots - 1 - j

        @pl.when(inside[i])
        def _():
            for u in range(per_slot):
                tile = ztbuf[tiles[0, 0, i * per_slot + u] + 1].astype(F32)
                limit = jnp.broadcast_to(counts[0, i], tile.shape)
                tile = jnp.where(limit > c * per_slot + u, tile, 0.0)
                own[i, :, u * rows:(u + 1) * rows] = tile.astype(BF16)

    for r in range(1, crow_count):
        pivot_copy(r).wait_recv()
    columns = pivots[0]
    for r in range(1, crow_count):
        columns = columns + pivots[r]

    turned = lanes_from(columns, owner, share, crow_count)
    state = 0.5 * (turned[:, :share] + turned.T[:share, :])
    row_id = lax.broadcasted_iota(jnp.int32, (share, width), 0)
    for first in range(0, share, PIVOTS):
        ids = range(PIVOTS)
        factors = [
            jnp.broadcast_to(state[:, first + q:first + q + 1], (share, width)) for q in ids
        ]
        small = [[factors[q][first + p:first + p + 1, :] for q in ids] for p in ids]
        left = [state[first + p:first + p + 1, :] for p in ids]
        right = [columns[first + p:first + p + 1, :] for p in ids]
        for q in ids:
            scale = lax.rsqrt(small[q][q])
            inverse = scale * scale
            panels[first + q:first + q + 1, :] = right[q] * scale
            small[q] = [x * inverse for x in small[q]]
            left[q] = left[q] * inverse[:, :share]
            right[q] = right[q] * inverse
            for p in ids:
                if p != q:
                    ratio = small[p][q]
                    small[p] = [x - ratio * y for x, y in zip(small[p], small[q])]
                    left[p] = left[p] - ratio[:, :share] * left[q]
                    right[p] = right[p] - ratio * right[q]
        for q in ids:
            state = state - factors[q][:, :share] * left[q]
            columns = columns - factors[q] * right[q]
        for q in ids:
            state = jnp.where(row_id[:, :share] == first + q, left[q], state)
            columns = jnp.where(row_id == first + q, right[q], columns)
    weights = columns.T
    w0, w1, w2 = thirds(weights)
    wide = jnp.concatenate([w0, w0, w1, w1, w0, w2], axis=1)

    square[:, :, :share] = panels[...].T.reshape(crow_count, share, share)
    panel_out[...] = square[c, :, :share]

    def red_copy(i, r):
        return pltpu.make_async_remote_copy(
            src_ref=reduced.at[i, peers[r]], dst_ref=partial.at[i, r],
            send_sem=red_send.at[i, r], recv_sem=red_recv.at[i, r],
            device_id={"crow": peers[r]}, device_id_type=MESH,
        )

    def scatter(i, part, pivot_rows):
        p0, p1, p2 = thirds(pivot_rows)
        part = part - dot(wide, jnp.concatenate([p0, p1, p0, p1, p2, p0], axis=0))
        reduced[i] = part.reshape(product.shape)
        for r in range(others):
            red_copy(i, r).start()

    def gather(i):
        result = reduced[i, c]
        for r in range(others):
            red_copy(i, r).wait_recv()
            result = result + partial[i, r]
        return result

    scatter(slots, gram, gram_pivot)

    for j in order:
        i = slots - 1 - j

        @pl.when(inside[i])
        def _():
            tile_copy(j).wait_recv()
            here = dot(own[i], arrived[i])
            product[...] = here.reshape(product.shape)
            scatter(i, here, product[owner])

    self_out[...] = gather(slots)
    for j in order:
        i = slots - 1 - j

        @pl.when(inside[i])
        def _():
            coupling_out[:, i * width:(i + 1) * width] = gather(i)

        @pl.when(jnp.logical_not(inside[i]))
        def _():
            coupling_out[:, i * width:(i + 1) * width] = jnp.zeros((share, width), F32)

    @pl.when(has_right)
    def _():
        halo(0).wait_send()
        halo(1).wait_send()

    @pl.when(has_left)
    def _():
        halo(2).wait_send()

    for r in range(1, crow_count):
        pivot_copy(r).wait_send()
        red_copy(slots, r - 1).wait_send()
    for j in range(slots):
        @pl.when(inside[j])
        def _():
            tile_copy(j).wait_send()
            for r in range(others):
                red_copy(j, r).wait_send()


def hand_over(a, b, c, a_out, b_out, c_out, sem):
    copies = [
        pltpu.make_async_copy(source, target, sem.at[k])
        for k, (source, target) in enumerate(((b, b_out), (a, a_out), (c, c_out)))
    ]
    for copy in copies:
        copy.start()
    for copy in copies:
        copy.wait()


def per_device(deflation, diag_op, upper_op, tile_blocks, pair_counts, pivot_owner):
    crow_count = lax.axis_size("crow")
    sub_count = lax.axis_size("sub")
    offsets = neighbour_offsets(min(16, sub_count // 2))
    blocks, rows = diag_op.shape[1], diag_op.shape[2]
    width = deflation.shape[2]
    slots = pair_counts.shape[1]
    per_slot = tile_blocks.shape[2] // slots
    share = width // crow_count
    others = crow_count - 1
    vmem = pl.BlockSpec(memory_space=pltpu.VMEM)
    smem = pl.BlockSpec(memory_space=pltpu.SMEM)
    hbm = pl.BlockSpec(memory_space=pltpu.HBM)
    dma = pltpu.SemaphoreType.DMA
    results = pl.pallas_call(
        functools.partial(kernel, offsets, sub_count, crow_count),
        out_shape=(
            pltpu.VMEM((share, width), F32),
            pltpu.VMEM((share, slots * width), F32),
            pltpu.VMEM((share, share), F32),
        ),
        in_specs=[hbm, hbm, hbm, smem, smem, smem],
        out_specs=(vmem, vmem, vmem),
        scratch_shapes=[
            pltpu.VMEM((blocks + 2, rows, width), BF16),
            pltpu.VMEM((blocks + 2, width, rows), BF16),
            pltpu.VMEM((blocks, rows, rows), BF16),
            pltpu.VMEM((blocks + 1, rows, rows), BF16),
            pltpu.VMEM((blocks, width, rows), BF16),
            pltpu.VMEM((slots, per_slot * rows, width), BF16),
            pltpu.VMEM((slots, per_slot * rows, width), BF16),
            pltpu.VMEM((slots, width, per_slot * rows), BF16),
            pltpu.VMEM((crow_count, share, width), F32),
            pltpu.VMEM((slots + 1, crow_count, share, width), F32),
            pltpu.VMEM((slots + 1, others, share, width), F32),
            pltpu.VMEM((crow_count, share, width), F32),
            pltpu.VMEM((crow_count, share, width), F32),
            pltpu.VMEM((share, width), F32),
            dma((3, 2)), dma((3,)), dma((3,)),
            dma((slots,)), dma((slots,)),
            dma((others,)), dma((others,)),
            dma((slots + 1, others)), dma((slots + 1, others)),
        ],
        compiler_params=pltpu.CompilerParams(
            collective_id=0, has_side_effects=True, vmem_limit_bytes=VMEM_BYTES
        ),
    )(
        deflation.reshape(blocks, rows, width),
        diag_op.reshape(blocks, rows, rows),
        upper_op.reshape(blocks, rows, rows),
        tile_blocks, pair_counts, pivot_owner,
    )
    return pl.pallas_call(
        hand_over,
        out_shape=tuple(jax.ShapeDtypeStruct(x.shape, F32) for x in results),
        in_specs=[vmem] * 3,
        out_specs=(hbm,) * 3,
        scratch_shapes=[dma((3,))],
        compiler_params=pltpu.CompilerParams(vmem_limit_bytes=2 * 1024 * 1024),
    )(*results)


def solution(mesh):
    placed = (
        P("sub", "crow", None),
        P("sub", "crow", None, None),
        P("sub", "crow", None, None),
        P("sub", "crow", None),
        P("sub", None),
        P("sub"),
    )
    return jax.shard_map(
        per_device,
        mesh=mesh,
        in_specs=placed,
        out_specs=(P(("sub", "crow"), None), P(("sub", "crow"), None), P(("sub", "crow"), None)),
        check_vma=False,
    )
```

```python
import functools

import jax
import jax.numpy as jnp
from jax import lax
from jax.experimental import pallas as pl
from jax.experimental.pallas import tpu as pltpu
from jax.sharding import PartitionSpec as P

MESH = pl.DeviceIdType.MESH
F32 = jnp.float32
BF16 = jnp.bfloat16
VMEM_BYTES = 56 * 1024 * 1024
PIVOTS = 4


def neighbour_offsets(across):
    return [-across - 1, -across, -across + 1, -1, 1, across - 1, across, across + 1]


def dot(a, b, dims=((1,), (0,)), precision=None):
    return lax.dot_general(a, b, (dims, ((), ())), precision=precision, preferred_element_type=F32)


def lanes_from(x, owner, share, parts):
    width = x.shape[1]
    chosen = jnp.broadcast_to(owner, x.shape)
    out = x
    for part in range(1, parts):
        out = jnp.where(chosen == part, pltpu.roll(x, width - part * share, 1), out)
    return out


def thirds(x):
    first = x.astype(BF16)
    rest = x - first.astype(F32)
    second = rest.astype(BF16)
    return first, second, (rest - second.astype(F32)).astype(BF16)


def kernel(
    offsets, sub_count, crow_count,
    z_hbm, d_hbm, u_hbm, tiles, counts, owners,
    self_out, coupling_out, panel_out,
    zbuf, ztbuf, dbuf, ubuf, abuf, outgoing, arrived, own, product, reduced, from_core, summed, from_far, pivots, square, panels,
    load_sem, halo_send, halo_recv, tile_send, tile_recv, pivot_send, pivot_recv, core_send, core_recv, far_send, far_recv,
):
    s = lax.axis_index("sub")
    c = lax.axis_index("crow")
    blocks = dbuf.shape[0]
    rows = dbuf.shape[1]
    width = zbuf.shape[2]
    slots = len(offsets)
    per_slot = outgoing.shape[1] // rows
    share = width // crow_count
    others = crow_count - 1
    peers = [lax.rem(c + r, crow_count) for r in range(1, crow_count)]
    inside = [jnp.logical_and(s + o >= 0, s + o < sub_count) for o in offsets]
    order = [k for pair in zip(range(slots), reversed(range(slots))) for k in pair][:slots]

    half = (blocks + 1) // 2
    loads = [
        pltpu.make_async_copy(
            source.at[pl.ds(first, count)], target.at[pl.ds(first + pad, count)], load_sem.at[k, h]
        )
        for h, (first, count) in enumerate(((0, half), (half, blocks - half)))
        for k, (source, target, pad) in enumerate(((z_hbm, zbuf, 1), (u_hbm, ubuf, 1), (d_hbm, dbuf, 0)))
    ]
    for load in loads:
        load.start()

    barrier = pltpu.get_barrier_semaphore()
    for peer in peers:
        pl.semaphore_signal(barrier, inc=1, device_id={"crow": peer}, device_id_type=MESH)
    expected = others
    for j in range(slots):
        @pl.when(inside[j])
        def _():
            pl.semaphore_signal(barrier, inc=1, device_id={"sub": s + offsets[j]}, device_id_type=MESH)
        expected = expected + jnp.where(inside[j], 1, 0)
    pl.semaphore_wait(barrier, expected)

    has_left, has_right = c > 0, c < crow_count - 1

    def halo(k):
        source, target, peer = (
            (z_hbm.at[blocks - 1], zbuf.at[0], c + 1),
            (u_hbm.at[blocks - 1], ubuf.at[0], c + 1),
            (z_hbm.at[0], zbuf.at[blocks + 1], c - 1),
        )[k]
        return pltpu.make_async_remote_copy(
            src_ref=source, dst_ref=target, send_sem=halo_send.at[k], recv_sem=halo_recv.at[k],
            device_id={"crow": peer}, device_id_type=MESH,
        )

    @pl.when(has_right)
    def _():
        halo(0).start()
        halo(1).start()

    @pl.when(has_left)
    def _():
        halo(2).start()

    @pl.when(jnp.logical_not(has_left))
    def _():
        zbuf[0] = jnp.zeros((rows, width), BF16)
        ubuf[0] = jnp.zeros((rows, rows), BF16)

    @pl.when(jnp.logical_not(has_right))
    def _():
        zbuf[blocks + 1] = jnp.zeros((rows, width), BF16)

    for load in loads:
        load.wait()

    unroll = max(n for n in range(1, 13) if blocks % n == 0)
    for k in range(unroll):
        ztbuf[1 + k] = zbuf[1 + k].T

    def apply(b):
        row = jnp.concatenate([dbuf[b], ubuf[b + 1]], axis=1)
        column = jnp.concatenate([zbuf[b + 1], zbuf[b + 2]], axis=0)
        total = dot(row, column) + dot(ubuf[b], zbuf[b], ((0,), (0,)))
        return total.astype(BF16)

    def apply_t(b):
        row = jnp.concatenate([ztbuf[b], ztbuf[b + 1]], axis=1)
        column = jnp.concatenate([ubuf[b], dbuf[b]], axis=0)
        total = dot(row, column) + dot(ztbuf[b + 2], ubuf[b + 1], ((1,), (1,)))
        return total.astype(BF16)

    @pl.when(has_left)
    def _():
        halo(0).wait_recv()
        halo(1).wait_recv()

    @pl.when(has_right)
    def _():
        halo(2).wait_recv()

    def tile_copy(j):
        return pltpu.make_async_remote_copy(
            src_ref=outgoing.at[j], dst_ref=arrived.at[slots - 1 - j],
            send_sem=tile_send.at[j], recv_sem=tile_recv.at[slots - 1 - j],
            device_id={"sub": s + offsets[j]}, device_id_type=MESH,
        )

    for j in order:
        @pl.when(inside[j])
        def _():
            for u in range(per_slot):
                outgoing[j, u * rows:(u + 1) * rows] = apply(tiles[0, 0, j * per_slot + u])
            tile_copy(j).start()

    @pl.loop(1, blocks // unroll)
    def _(step):
        for k in range(unroll):
            b = 1 + step * unroll + k
            ztbuf[b] = zbuf[b].T

    ztbuf[0] = zbuf[0].T
    ztbuf[blocks + 1] = zbuf[blocks + 1].T

    @pl.loop(0, blocks // unroll)
    def _(step):
        for k in range(unroll):
            b = step * unroll + k
            abuf[b] = apply_t(b)

    gram_t = jnp.zeros((width, width), F32)
    for first in range(0, blocks, unroll):
        left = jnp.concatenate([abuf[first + k] for k in range(unroll)], axis=1)
        right = zbuf[first + 1:first + 1 + unroll].reshape(unroll * rows, width)
        gram_t = gram_t + dot(left, right)
    square[...] = gram_t.reshape(square.shape)
    owner = owners[0]
    pivots[0] = square[owner]

    def pivot_copy(r):
        return pltpu.make_async_remote_copy(
            src_ref=pivots.at[0], dst_ref=pivots.at[r],
            send_sem=pivot_send.at[r - 1], recv_sem=pivot_recv.at[r - 1],
            device_id={"crow": peers[r - 1]}, device_id_type=MESH,
        )

    for r in range(1, crow_count):
        pivot_copy(r).start()

    gram = gram_t.T
    product[...] = gram.reshape(product.shape)
    gram_pivot = product[owner]
    for j in order:
        i = slots - 1 - j

        @pl.when(inside[i])
        def _():
            for u in range(per_slot):
                tile = ztbuf[tiles[0, 0, i * per_slot + u] + 1].astype(F32)
                limit = jnp.broadcast_to(counts[0, i], tile.shape)
                tile = jnp.where(limit > c * per_slot + u, tile, 0.0)
                own[i, :, u * rows:(u + 1) * rows] = tile.astype(BF16)

    for r in range(1, crow_count):
        pivot_copy(r).wait_recv()
    columns = pivots[0]
    for r in range(1, crow_count):
        columns = columns + pivots[r]

    turned = lanes_from(columns, owner, share, crow_count)
    state = 0.5 * (turned[:, :share] + turned.T[:share, :])
    row_id = lax.broadcasted_iota(jnp.int32, (share, width), 0)
    for first in range(0, share, PIVOTS):
        ids = range(PIVOTS)
        factors = [
            jnp.broadcast_to(state[:, first + q:first + q + 1], (share, width)) for q in ids
        ]
        small = [[factors[q][first + p:first + p + 1, :] for q in ids] for p in ids]
        left = [state[first + p:first + p + 1, :] for p in ids]
        right = [columns[first + p:first + p + 1, :] for p in ids]
        for q in ids:
            scale = lax.rsqrt(small[q][q])
            inverse = scale * scale
            panels[first + q:first + q + 1, :] = right[q] * scale
            small[q] = [x * inverse for x in small[q]]
            left[q] = left[q] * inverse[:, :share]
            right[q] = right[q] * inverse
            for p in ids:
                if p != q:
                    ratio = small[p][q]
                    small[p] = [x - ratio * y for x, y in zip(small[p], small[q])]
                    left[p] = left[p] - ratio[:, :share] * left[q]
                    right[p] = right[p] - ratio * right[q]
        for q in ids:
            state = state - factors[q][:, :share] * left[q]
            columns = columns - factors[q] * right[q]
        for q in ids:
            state = jnp.where(row_id[:, :share] == first + q, left[q], state)
            columns = jnp.where(row_id == first + q, right[q], columns)
    weights = columns.T
    w0, w1, w2 = thirds(weights)
    wide = jnp.concatenate([w0, w0, w1, w1, w0, w2], axis=1)

    square[:, :, :share] = panels[...].T.reshape(crow_count, share, share)
    panel_out[...] = square[c, :, :share]

    half_place, pair_place = lax.rem(c, 2), lax.div(c, 2)

    def core_copy(i):
        return pltpu.make_async_remote_copy(
            src_ref=reduced.at[i, 1 - half_place], dst_ref=from_core.at[i],
            send_sem=core_send.at[i], recv_sem=core_recv.at[i],
            device_id={"crow": c + 1 - 2 * half_place}, device_id_type=MESH,
        )

    def far_copy(i):
        return pltpu.make_async_remote_copy(
            src_ref=summed.at[i, 1 - pair_place], dst_ref=from_far.at[i],
            send_sem=far_send.at[i], recv_sem=far_recv.at[i],
            device_id={"crow": c + 2 - 4 * pair_place}, device_id_type=MESH,
        )

    def scatter(i, part, pivot_rows):
        p0, p1, p2 = thirds(pivot_rows)
        part = part - dot(wide, jnp.concatenate([p0, p1, p0, p1, p2, p0], axis=0))
        for place in range(crow_count):
            reduced[i, place % 2, place // 2] = part[place * share:(place + 1) * share]
        core_copy(i).start()

    def pass_on(i):
        core_copy(i).wait_recv()
        summed[i] = reduced[i, half_place] + from_core[i]
        far_copy(i).start()

    def gather(i):
        far_copy(i).wait_recv()
        return summed[i, pair_place] + from_far[i]

    scatter(slots, gram, gram_pivot)

    for j in order:
        i = slots - 1 - j

        @pl.when(inside[i])
        def _():
            tile_copy(j).wait_recv()
            here = dot(own[i], arrived[i])
            product[...] = here.reshape(product.shape)
            scatter(i, here, product[owner])

    pass_on(slots)
    for j in order:
        @pl.when(inside[slots - 1 - j])
        def _():
            pass_on(slots - 1 - j)

    self_out[...] = gather(slots)
    for j in order:
        i = slots - 1 - j

        @pl.when(inside[i])
        def _():
            coupling_out[:, i * width:(i + 1) * width] = gather(i)

        @pl.when(jnp.logical_not(inside[i]))
        def _():
            coupling_out[:, i * width:(i + 1) * width] = jnp.zeros((share, width), F32)

    @pl.when(has_right)
    def _():
        halo(0).wait_send()
        halo(1).wait_send()

    @pl.when(has_left)
    def _():
        halo(2).wait_send()

    for r in range(1, crow_count):
        pivot_copy(r).wait_send()
    core_copy(slots).wait_send()
    far_copy(slots).wait_send()
    for j in range(slots):
        @pl.when(inside[j])
        def _():
            tile_copy(j).wait_send()
            core_copy(j).wait_send()
            far_copy(j).wait_send()


def hand_over(a, b, c, a_out, b_out, c_out, sem):
    copies = [
        pltpu.make_async_copy(source, target, sem.at[k])
        for k, (source, target) in enumerate(((b, b_out), (a, a_out), (c, c_out)))
    ]
    for copy in copies:
        copy.start()
    for copy in copies:
        copy.wait()


def per_device(deflation, diag_op, upper_op, tile_blocks, pair_counts, pivot_owner):
    crow_count = lax.axis_size("crow")
    sub_count = lax.axis_size("sub")
    offsets = neighbour_offsets(min(16, sub_count // 2))
    blocks, rows = diag_op.shape[1], diag_op.shape[2]
    width = deflation.shape[2]
    slots = pair_counts.shape[1]
    per_slot = tile_blocks.shape[2] // slots
    share = width // crow_count
    others = crow_count - 1
    vmem = pl.BlockSpec(memory_space=pltpu.VMEM)
    smem = pl.BlockSpec(memory_space=pltpu.SMEM)
    hbm = pl.BlockSpec(memory_space=pltpu.HBM)
    dma = pltpu.SemaphoreType.DMA
    results = pl.pallas_call(
        functools.partial(kernel, offsets, sub_count, crow_count),
        out_shape=(
            pltpu.VMEM((share, width), F32),
            pltpu.VMEM((share, slots * width), F32),
            pltpu.VMEM((share, share), F32),
        ),
        in_specs=[hbm, hbm, hbm, smem, smem, smem],
        out_specs=(vmem, vmem, vmem),
        scratch_shapes=[
            pltpu.VMEM((blocks + 2, rows, width), BF16),
            pltpu.VMEM((blocks + 2, width, rows), BF16),
            pltpu.VMEM((blocks, rows, rows), BF16),
            pltpu.VMEM((blocks + 1, rows, rows), BF16),
            pltpu.VMEM((blocks, width, rows), BF16),
            pltpu.VMEM((slots, per_slot * rows, width), BF16),
            pltpu.VMEM((slots, per_slot * rows, width), BF16),
            pltpu.VMEM((slots, width, per_slot * rows), BF16),
            pltpu.VMEM((crow_count, share, width), F32),
            pltpu.VMEM((slots + 1, 2, 2, share, width), F32),
            pltpu.VMEM((slots + 1, 2, share, width), F32),
            pltpu.VMEM((slots + 1, 2, share, width), F32),
            pltpu.VMEM((slots + 1, share, width), F32),
            pltpu.VMEM((crow_count, share, width), F32),
            pltpu.VMEM((crow_count, share, width), F32),
            pltpu.VMEM((share, width), F32),
            dma((3, 2)), dma((3,)), dma((3,)),
            dma((slots,)), dma((slots,)),
            dma((others,)), dma((others,)),
            dma((slots + 1,)), dma((slots + 1,)), dma((slots + 1,)), dma((slots + 1,)),
        ],
        compiler_params=pltpu.CompilerParams(
            collective_id=0, has_side_effects=True, vmem_limit_bytes=VMEM_BYTES
        ),
    )(
        deflation.reshape(blocks, rows, width),
        diag_op.reshape(blocks, rows, rows),
        upper_op.reshape(blocks, rows, rows),
        tile_blocks, pair_counts, pivot_owner,
    )
    return pl.pallas_call(
        hand_over,
        out_shape=tuple(jax.ShapeDtypeStruct(x.shape, F32) for x in results),
        in_specs=[vmem] * 3,
        out_specs=(hbm,) * 3,
        scratch_shapes=[dma((3,))],
        compiler_params=pltpu.CompilerParams(vmem_limit_bytes=2 * 1024 * 1024),
    )(*results)


def solution(mesh):
    placed = (
        P("sub", "crow", None),
        P("sub", "crow", None, None),
        P("sub", "crow", None, None),
        P("sub", "crow", None),
        P("sub", None),
        P("sub"),
    )
    return jax.shard_map(
        per_device,
        mesh=mesh,
        in_specs=placed,
        out_specs=(P(("sub", "crow"), None), P(("sub", "crow"), None), P(("sub", "crow"), None)),
        check_vma=False,
    )
```

```python
import functools

import jax
import jax.numpy as jnp
from jax import lax
from jax.experimental import pallas as pl
from jax.experimental.pallas import tpu as pltpu
from jax.sharding import PartitionSpec as P

MESH = pl.DeviceIdType.MESH
F32 = jnp.float32
BF16 = jnp.bfloat16
VMEM_BYTES = 56 * 1024 * 1024
PIVOTS = 4


def neighbour_offsets(across):
    return [-across - 1, -across, -across + 1, -1, 1, across - 1, across, across + 1]


def dot(a, b, dims=((1,), (0,)), precision=None):
    return lax.dot_general(a, b, (dims, ((), ())), precision=precision, preferred_element_type=F32)


def lanes_from(x, owner, share, parts):
    width = x.shape[1]
    chosen = jnp.broadcast_to(owner, x.shape)
    out = x
    for part in range(1, parts):
        out = jnp.where(chosen == part, pltpu.roll(x, width - part * share, 1), out)
    return out


def thirds(x):
    first = x.astype(BF16)
    rest = x - first.astype(F32)
    second = rest.astype(BF16)
    return first, second, (rest - second.astype(F32)).astype(BF16)


def kernel(
    offsets, sub_count, crow_count,
    z_hbm, d_hbm, u_hbm, tiles, counts, owners,
    self_out, coupling_out, panel_out,
    zbuf, ztbuf, dbuf, ubuf, abuf, outgoing, arrived, own, product, reduced, from_core, summed, from_far, pivots, square, panels,
    load_sem, halo_send, halo_recv, tile_send, tile_recv, pivot_send, pivot_recv, core_send, core_recv, far_send, far_recv,
):
    s = lax.axis_index("sub")
    c = lax.axis_index("crow")
    blocks = dbuf.shape[0]
    rows = dbuf.shape[1]
    width = zbuf.shape[2]
    slots = len(offsets)
    per_slot = outgoing.shape[1] // rows
    share = width // crow_count
    others = crow_count - 1
    peers = [lax.rem(c + r, crow_count) for r in range(1, crow_count)]
    inside = [jnp.logical_and(s + o >= 0, s + o < sub_count) for o in offsets]
    order = [k for pair in zip(range(slots), reversed(range(slots))) for k in pair][:slots]

    half = (blocks + 1) // 2
    loads = [
        pltpu.make_async_copy(
            source.at[pl.ds(first, count)], target.at[pl.ds(first + pad, count)], load_sem.at[k, h]
        )
        for h, (first, count) in enumerate(((0, half), (half, blocks - half)))
        for k, (source, target, pad) in enumerate(((z_hbm, zbuf, 1), (u_hbm, ubuf, 1), (d_hbm, dbuf, 0)))
    ]
    barrier = pltpu.get_barrier_semaphore()
    for peer in peers:
        pl.semaphore_signal(barrier, inc=1, device_id={"crow": peer}, device_id_type=MESH)
    expected = others
    for j in range(slots):
        @pl.when(inside[j])
        def _():
            pl.semaphore_signal(barrier, inc=1, device_id={"sub": s + offsets[j]}, device_id_type=MESH)
        expected = expected + jnp.where(inside[j], 1, 0)
    for load in loads:
        load.start()
    pl.semaphore_wait(barrier, expected)

    has_left, has_right = c > 0, c < crow_count - 1

    def halo(k):
        source, target, peer = (
            (z_hbm.at[blocks - 1], zbuf.at[0], c + 1),
            (u_hbm.at[blocks - 1], ubuf.at[0], c + 1),
            (z_hbm.at[0], zbuf.at[blocks + 1], c - 1),
        )[k]
        return pltpu.make_async_remote_copy(
            src_ref=source, dst_ref=target, send_sem=halo_send.at[k], recv_sem=halo_recv.at[k],
            device_id={"crow": peer}, device_id_type=MESH,
        )

    @pl.when(has_right)
    def _():
        halo(0).start()
        halo(1).start()

    @pl.when(has_left)
    def _():
        halo(2).start()

    @pl.when(jnp.logical_not(has_left))
    def _():
        zbuf[0] = jnp.zeros((rows, width), BF16)
        ubuf[0] = jnp.zeros((rows, rows), BF16)

    @pl.when(jnp.logical_not(has_right))
    def _():
        zbuf[blocks + 1] = jnp.zeros((rows, width), BF16)

    for load in loads:
        load.wait()

    unroll = max(n for n in range(1, 13) if blocks % n == 0)
    for k in range(unroll):
        ztbuf[1 + k] = zbuf[1 + k].T

    def apply(b):
        row = jnp.concatenate([dbuf[b], ubuf[b + 1]], axis=1)
        column = jnp.concatenate([zbuf[b + 1], zbuf[b + 2]], axis=0)
        total = dot(row, column) + dot(ubuf[b], zbuf[b], ((0,), (0,)))
        return total.astype(BF16)

    def apply_t(b):
        row = jnp.concatenate([ztbuf[b], ztbuf[b + 1]], axis=1)
        column = jnp.concatenate([ubuf[b], dbuf[b]], axis=0)
        total = dot(row, column) + dot(ztbuf[b + 2], ubuf[b + 1], ((1,), (1,)))
        return total.astype(BF16)

    @pl.when(has_left)
    def _():
        halo(0).wait_recv()
        halo(1).wait_recv()

    @pl.when(has_right)
    def _():
        halo(2).wait_recv()

    def tile_copy(j, u):
        here = pl.ds(u * rows, rows)
        return pltpu.make_async_remote_copy(
            src_ref=outgoing.at[j, here], dst_ref=arrived.at[slots - 1 - j, here],
            send_sem=tile_send.at[j, u], recv_sem=tile_recv.at[slots - 1 - j, u],
            device_id={"sub": s + offsets[j]}, device_id_type=MESH,
        )

    for j in order:
        @pl.when(inside[j])
        def _():
            for u in range(per_slot):
                outgoing[j, u * rows:(u + 1) * rows] = apply(tiles[0, 0, j * per_slot + u])
                tile_copy(j, u).start()

    @pl.loop(1, blocks // unroll)
    def _(step):
        for k in range(unroll):
            b = 1 + step * unroll + k
            ztbuf[b] = zbuf[b].T

    ztbuf[0] = zbuf[0].T
    ztbuf[blocks + 1] = zbuf[blocks + 1].T

    @pl.loop(0, blocks // unroll)
    def _(step):
        for k in range(unroll):
            b = step * unroll + k
            abuf[b] = apply_t(b)

    gram_t = jnp.zeros((width, width), F32)
    for first in range(0, blocks, unroll):
        left = jnp.concatenate([abuf[first + k] for k in range(unroll)], axis=1)
        right = zbuf[first + 1:first + 1 + unroll].reshape(unroll * rows, width)
        gram_t = gram_t + dot(left, right)
    square[...] = gram_t.reshape(square.shape)
    owner = owners[0]
    pivots[0] = square[owner]

    def pivot_copy(r):
        return pltpu.make_async_remote_copy(
            src_ref=pivots.at[0], dst_ref=pivots.at[r],
            send_sem=pivot_send.at[r - 1], recv_sem=pivot_recv.at[r - 1],
            device_id={"crow": peers[r - 1]}, device_id_type=MESH,
        )

    for r in range(1, crow_count):
        pivot_copy(r).start()

    gram = gram_t.T
    product[...] = gram.reshape(product.shape)
    gram_pivot = product[owner]
    for j in order:
        i = slots - 1 - j

        @pl.when(inside[i])
        def _():
            for u in range(per_slot):
                tile = ztbuf[tiles[0, 0, i * per_slot + u] + 1].astype(F32)
                limit = jnp.broadcast_to(counts[0, i], tile.shape)
                tile = jnp.where(limit > c * per_slot + u, tile, 0.0)
                own[i, :, u * rows:(u + 1) * rows] = tile.astype(BF16)

    for r in range(1, crow_count):
        pivot_copy(r).wait_recv()
    columns = pivots[0]
    for r in range(1, crow_count):
        columns = columns + pivots[r]

    turned = lanes_from(columns, owner, share, crow_count)
    state = 0.5 * (turned[:, :share] + turned.T[:share, :])
    row_id = lax.broadcasted_iota(jnp.int32, (share, width), 0)
    for first in range(0, share, PIVOTS):
        ids = range(PIVOTS)
        factors = [
            jnp.broadcast_to(state[:, first + q:first + q + 1], (share, width)) for q in ids
        ]
        small = [[factors[q][first + p:first + p + 1, :] for q in ids] for p in ids]
        left = [state[first + p:first + p + 1, :] for p in ids]
        right = [columns[first + p:first + p + 1, :] for p in ids]
        for q in ids:
            scale = lax.rsqrt(small[q][q])
            inverse = scale * scale
            panels[first + q:first + q + 1, :] = right[q] * scale
            small[q] = [x * inverse for x in small[q]]
            left[q] = left[q] * inverse[:, :share]
            right[q] = right[q] * inverse
            for p in ids:
                if p != q:
                    ratio = small[p][q]
                    small[p] = [x - ratio * y for x, y in zip(small[p], small[q])]
                    left[p] = left[p] - ratio[:, :share] * left[q]
                    right[p] = right[p] - ratio * right[q]
        for q in ids:
            state = state - factors[q][:, :share] * left[q]
            columns = columns - factors[q] * right[q]
        for q in ids:
            state = jnp.where(row_id[:, :share] == first + q, left[q], state)
            columns = jnp.where(row_id == first + q, right[q], columns)
    weights = columns.T
    w0, w1, w2 = thirds(weights)
    wide = jnp.concatenate([w0, w0, w1, w1, w0, w2], axis=1)

    square[:, :, :share] = panels[...].T.reshape(crow_count, share, share)
    panel_out[...] = square[c, :, :share]

    half_place, pair_place = lax.rem(c, 2), lax.div(c, 2)

    def core_copy(i):
        return pltpu.make_async_remote_copy(
            src_ref=reduced.at[i, 1 - half_place], dst_ref=from_core.at[i],
            send_sem=core_send.at[i], recv_sem=core_recv.at[i],
            device_id={"crow": c + 1 - 2 * half_place}, device_id_type=MESH,
        )

    def far_copy(i):
        return pltpu.make_async_remote_copy(
            src_ref=summed.at[i, 1 - pair_place], dst_ref=from_far.at[i],
            send_sem=far_send.at[i], recv_sem=far_recv.at[i],
            device_id={"crow": c + 2 - 4 * pair_place}, device_id_type=MESH,
        )

    def scatter(i, part, pivot_rows):
        p0, p1, p2 = thirds(pivot_rows)
        part = part - dot(wide, jnp.concatenate([p0, p1, p0, p1, p2, p0], axis=0))
        for place in range(crow_count):
            reduced[i, place % 2, place // 2] = part[place * share:(place + 1) * share]
        core_copy(i).start()

    def pass_on(i):
        core_copy(i).wait_recv()
        summed[i] = reduced[i, half_place] + from_core[i]
        far_copy(i).start()

    def gather(i):
        far_copy(i).wait_recv()
        return summed[i, pair_place] + from_far[i]

    scatter(slots, gram, gram_pivot)

    for j in order[::-1]:
        i = slots - 1 - j

        @pl.when(inside[i])
        def _():
            for u in range(per_slot):
                tile_copy(j, u).wait_recv()
            here = dot(own[i], arrived[i])
            product[...] = here.reshape(product.shape)
            scatter(i, here, product[owner])

    pass_on(slots)
    for j in order[::-1]:
        @pl.when(inside[slots - 1 - j])
        def _():
            pass_on(slots - 1 - j)

    self_out[...] = gather(slots)
    for j in order:
        i = slots - 1 - j

        @pl.when(inside[i])
        def _():
            coupling_out[:, i * width:(i + 1) * width] = gather(i)

        @pl.when(jnp.logical_not(inside[i]))
        def _():
            coupling_out[:, i * width:(i + 1) * width] = jnp.zeros((share, width), F32)

    @pl.when(has_right)
    def _():
        halo(0).wait_send()
        halo(1).wait_send()

    @pl.when(has_left)
    def _():
        halo(2).wait_send()

    for r in range(1, crow_count):
        pivot_copy(r).wait_send()
    core_copy(slots).wait_send()
    far_copy(slots).wait_send()
    for j in range(slots):
        @pl.when(inside[j])
        def _():
            for u in range(per_slot):
                tile_copy(j, u).wait_send()
            core_copy(j).wait_send()
            far_copy(j).wait_send()


def hand_over(a, b, c, a_out, b_out, c_out, sem):
    copies = [
        pltpu.make_async_copy(source, target, sem.at[k])
        for k, (source, target) in enumerate(((b, b_out), (a, a_out), (c, c_out)))
    ]
    for copy in copies:
        copy.start()
    for copy in copies:
        copy.wait()


def per_device(deflation, diag_op, upper_op, tile_blocks, pair_counts, pivot_owner):
    crow_count = lax.axis_size("crow")
    sub_count = lax.axis_size("sub")
    offsets = neighbour_offsets(min(16, sub_count // 2))
    blocks, rows = diag_op.shape[1], diag_op.shape[2]
    width = deflation.shape[2]
    slots = pair_counts.shape[1]
    per_slot = tile_blocks.shape[2] // slots
    share = width // crow_count
    others = crow_count - 1
    vmem = pl.BlockSpec(memory_space=pltpu.VMEM)
    smem = pl.BlockSpec(memory_space=pltpu.SMEM)
    hbm = pl.BlockSpec(memory_space=pltpu.HBM)
    dma = pltpu.SemaphoreType.DMA
    results = pl.pallas_call(
        functools.partial(kernel, offsets, sub_count, crow_count),
        out_shape=(
            pltpu.VMEM((share, width), F32),
            pltpu.VMEM((share, slots * width), F32),
            pltpu.VMEM((share, share), F32),
        ),
        in_specs=[hbm, hbm, hbm, smem, smem, smem],
        out_specs=(vmem, vmem, vmem),
        scratch_shapes=[
            pltpu.VMEM((blocks + 2, rows, width), BF16),
            pltpu.VMEM((blocks + 2, width, rows), BF16),
            pltpu.VMEM((blocks, rows, rows), BF16),
            pltpu.VMEM((blocks + 1, rows, rows), BF16),
            pltpu.VMEM((blocks, width, rows), BF16),
            pltpu.VMEM((slots, per_slot * rows, width), BF16),
            pltpu.VMEM((slots, per_slot * rows, width), BF16),
            pltpu.VMEM((slots, width, per_slot * rows), BF16),
            pltpu.VMEM((crow_count, share, width), F32),
            pltpu.VMEM((slots + 1, 2, 2, share, width), F32),
            pltpu.VMEM((slots + 1, 2, share, width), F32),
            pltpu.VMEM((slots + 1, 2, share, width), F32),
            pltpu.VMEM((slots + 1, share, width), F32),
            pltpu.VMEM((crow_count, share, width), F32),
            pltpu.VMEM((crow_count, share, width), F32),
            pltpu.VMEM((share, width), F32),
            dma((3, 2)), dma((3,)), dma((3,)),
            dma((slots, per_slot)), dma((slots, per_slot)),
            dma((others,)), dma((others,)),
            dma((slots + 1,)), dma((slots + 1,)), dma((slots + 1,)), dma((slots + 1,)),
        ],
        compiler_params=pltpu.CompilerParams(
            collective_id=0, has_side_effects=True, vmem_limit_bytes=VMEM_BYTES
        ),
    )(
        deflation.reshape(blocks, rows, width),
        diag_op.reshape(blocks, rows, rows),
        upper_op.reshape(blocks, rows, rows),
        tile_blocks, pair_counts, pivot_owner,
    )
    return pl.pallas_call(
        hand_over,
        out_shape=tuple(jax.ShapeDtypeStruct(x.shape, F32) for x in results),
        in_specs=[vmem] * 3,
        out_specs=(hbm,) * 3,
        scratch_shapes=[dma((3,))],
        compiler_params=pltpu.CompilerParams(vmem_limit_bytes=2 * 1024 * 1024),
    )(*results)


def solution(mesh):
    placed = (
        P("sub", "crow", None),
        P("sub", "crow", None, None),
        P("sub", "crow", None, None),
        P("sub", "crow", None),
        P("sub", None),
        P("sub"),
    )
    return jax.shard_map(
        per_device,
        mesh=mesh,
        in_specs=placed,
        out_specs=(P(("sub", "crow"), None), P(("sub", "crow"), None), P(("sub", "crow"), None)),
        check_vma=False,
    )
```

```python
import functools

import jax
import jax.numpy as jnp
from jax import lax
from jax.experimental import pallas as pl
from jax.experimental.pallas import tpu as pltpu
from jax.sharding import PartitionSpec as P

MESH = pl.DeviceIdType.MESH
F32 = jnp.float32
BF16 = jnp.bfloat16
VMEM_BYTES = 56 * 1024 * 1024
PIVOTS = 4


def neighbour_offsets(across):
    return [-across - 1, -across, -across + 1, -1, 1, across - 1, across, across + 1]


def dot(a, b, dims=((1,), (0,)), precision=None):
    return lax.dot_general(a, b, (dims, ((), ())), precision=precision, preferred_element_type=F32)


def lanes_from(x, owner, share, parts):
    width = x.shape[1]
    chosen = jnp.broadcast_to(owner, x.shape)
    out = x
    for part in range(1, parts):
        out = jnp.where(chosen == part, pltpu.roll(x, width - part * share, 1), out)
    return out


def thirds(x):
    first = x.astype(BF16)
    rest = x - first.astype(F32)
    second = rest.astype(BF16)
    return first, second, (rest - second.astype(F32)).astype(BF16)


def kernel(
    offsets, sub_count, crow_count,
    z_hbm, d_hbm, u_hbm, tiles, counts, owners,
    self_out, coupling_out, panel_out,
    zbuf, ztbuf, dbuf, ubuf, abuf, outgoing, arrived, own, product, reduced, from_core, summed, from_far, pivots, square, panels,
    load_sem, halo_send, halo_recv, tile_send, tile_recv, pivot_send, pivot_recv, core_send, core_recv, far_send, far_recv,
):
    s = lax.axis_index("sub")
    c = lax.axis_index("crow")
    blocks = dbuf.shape[0]
    rows = dbuf.shape[1]
    width = zbuf.shape[2]
    slots = len(offsets)
    per_slot = outgoing.shape[1] // rows
    share = width // crow_count
    others = crow_count - 1
    peers = [lax.rem(c + r, crow_count) for r in range(1, crow_count)]
    inside = [jnp.logical_and(s + o >= 0, s + o < sub_count) for o in offsets]
    order = [k for pair in zip(range(slots), reversed(range(slots))) for k in pair][:slots]

    half = (blocks + 1) // 2
    loads = [
        pltpu.make_async_copy(
            source.at[pl.ds(first, count)], target.at[pl.ds(first + pad, count)], load_sem.at[k, h]
        )
        for h, (first, count) in enumerate(((0, half), (half, blocks - half)))
        for k, (source, target, pad) in enumerate(((z_hbm, zbuf, 1), (u_hbm, ubuf, 1), (d_hbm, dbuf, 0)))
    ]
    barrier = pltpu.get_barrier_semaphore()
    for peer in peers:
        pl.semaphore_signal(barrier, inc=1, device_id={"crow": peer}, device_id_type=MESH)
    expected = others
    for j in range(slots):
        @pl.when(inside[j])
        def _():
            pl.semaphore_signal(barrier, inc=1, device_id={"sub": s + offsets[j]}, device_id_type=MESH)
        expected = expected + jnp.where(inside[j], 1, 0)
    for load in loads:
        load.start()
    pl.semaphore_wait(barrier, expected)

    has_left, has_right = c > 0, c < crow_count - 1

    def halo(k):
        source, target, peer = (
            (z_hbm.at[blocks - 1], zbuf.at[0], c + 1),
            (u_hbm.at[blocks - 1], ubuf.at[0], c + 1),
            (z_hbm.at[0], zbuf.at[blocks + 1], c - 1),
        )[k]
        return pltpu.make_async_remote_copy(
            src_ref=source, dst_ref=target, send_sem=halo_send.at[k], recv_sem=halo_recv.at[k],
            device_id={"crow": peer}, device_id_type=MESH,
        )

    @pl.when(has_right)
    def _():
        halo(0).start()
        halo(1).start()

    @pl.when(has_left)
    def _():
        halo(2).start()

    @pl.when(jnp.logical_not(has_left))
    def _():
        zbuf[0] = jnp.zeros((rows, width), BF16)
        ubuf[0] = jnp.zeros((rows, rows), BF16)

    @pl.when(jnp.logical_not(has_right))
    def _():
        zbuf[blocks + 1] = jnp.zeros((rows, width), BF16)

    for load in loads:
        load.wait()

    unroll = max(n for n in range(1, 13) if blocks % n == 0)
    for k in range(unroll):
        ztbuf[1 + k] = zbuf[1 + k].T

    def apply(b):
        row = jnp.concatenate([dbuf[b], ubuf[b + 1]], axis=1)
        column = jnp.concatenate([zbuf[b + 1], zbuf[b + 2]], axis=0)
        total = dot(row, column) + dot(ubuf[b], zbuf[b], ((0,), (0,)))
        return total.astype(BF16)

    def apply_t(b):
        row = jnp.concatenate([ztbuf[b], ztbuf[b + 1]], axis=1)
        column = jnp.concatenate([ubuf[b], dbuf[b]], axis=0)
        total = dot(row, column) + dot(ztbuf[b + 2], ubuf[b + 1], ((1,), (1,)))
        return total.astype(BF16)

    @pl.when(has_left)
    def _():
        halo(0).wait_recv()
        halo(1).wait_recv()

    @pl.when(has_right)
    def _():
        halo(2).wait_recv()

    def tile_copy(j):
        return pltpu.make_async_remote_copy(
            src_ref=outgoing.at[j], dst_ref=arrived.at[slots - 1 - j],
            send_sem=tile_send.at[j], recv_sem=tile_recv.at[slots - 1 - j],
            device_id={"sub": s + offsets[j]}, device_id_type=MESH,
        )

    for j in order:
        @pl.when(inside[j])
        def _():
            for u in range(per_slot):
                outgoing[j, u * rows:(u + 1) * rows] = apply(tiles[0, 0, j * per_slot + u])
            tile_copy(j).start()

    @pl.loop(1, blocks // unroll)
    def _(step):
        for k in range(unroll):
            b = 1 + step * unroll + k
            ztbuf[b] = zbuf[b].T

    ztbuf[0] = zbuf[0].T
    ztbuf[blocks + 1] = zbuf[blocks + 1].T

    @pl.loop(0, blocks // unroll)
    def _(step):
        for k in range(unroll):
            b = step * unroll + k
            abuf[b] = apply_t(b)

    gram_t = jnp.zeros((width, width), F32)
    for first in range(0, blocks, unroll):
        left = jnp.concatenate([abuf[first + k] for k in range(unroll)], axis=1)
        right = zbuf[first + 1:first + 1 + unroll].reshape(unroll * rows, width)
        gram_t = gram_t + dot(left, right)
    square[...] = gram_t.reshape(square.shape)
    owner = owners[0]
    pivots[0] = square[owner]

    def pivot_copy(r):
        return pltpu.make_async_remote_copy(
            src_ref=pivots.at[0], dst_ref=pivots.at[r],
            send_sem=pivot_send.at[r - 1], recv_sem=pivot_recv.at[r - 1],
            device_id={"crow": peers[r - 1]}, device_id_type=MESH,
        )

    for r in range(1, crow_count):
        pivot_copy(r).start()

    gram = gram_t.T
    product[...] = gram.reshape(product.shape)
    gram_pivot = product[owner]
    for j in order:
        i = slots - 1 - j

        @pl.when(inside[i])
        def _():
            for u in range(per_slot):
                tile = ztbuf[tiles[0, 0, i * per_slot + u] + 1].astype(F32)
                limit = jnp.broadcast_to(counts[0, i], tile.shape)
                tile = jnp.where(limit > c * per_slot + u, tile, 0.0)
                own[i, :, u * rows:(u + 1) * rows] = tile.astype(BF16)

    for r in range(1, crow_count):
        pivot_copy(r).wait_recv()
    columns = pivots[0]
    for r in range(1, crow_count):
        columns = columns + pivots[r]

    turned = lanes_from(columns, owner, share, crow_count)
    state = 0.5 * (turned[:, :share] + turned.T[:share, :])
    row_id = lax.broadcasted_iota(jnp.int32, (share, width), 0)
    for first in range(0, share, PIVOTS):
        ids = range(PIVOTS)
        factors = [
            jnp.broadcast_to(state[:, first + q:first + q + 1], (share, width)) for q in ids
        ]
        small = [[factors[q][first + p:first + p + 1, :] for q in ids] for p in ids]
        left = [state[first + p:first + p + 1, :] for p in ids]
        right = [columns[first + p:first + p + 1, :] for p in ids]
        for q in ids:
            scale = lax.rsqrt(small[q][q])
            inverse = scale * scale
            panels[first + q:first + q + 1, :] = right[q] * scale
            small[q] = [x * inverse for x in small[q]]
            left[q] = left[q] * inverse[:, :share]
            right[q] = right[q] * inverse
            for p in ids:
                if p != q:
                    ratio = small[p][q]
                    small[p] = [x - ratio * y for x, y in zip(small[p], small[q])]
                    left[p] = left[p] - ratio[:, :share] * left[q]
                    right[p] = right[p] - ratio * right[q]
        for q in ids:
            state = state - factors[q][:, :share] * left[q]
            columns = columns - factors[q] * right[q]
        for q in ids:
            state = jnp.where(row_id[:, :share] == first + q, left[q], state)
            columns = jnp.where(row_id == first + q, right[q], columns)
    weights = columns.T
    w0, w1, w2 = thirds(weights)
    wide = jnp.concatenate([w0, w0, w1, w1, w0, w2], axis=1)

    square[:, :, :share] = panels[...].T.reshape(crow_count, share, share)
    panel_out[...] = square[c, :, :share]

    half_place, pair_place = lax.rem(c, 2), lax.div(c, 2)

    def core_copy(i):
        return pltpu.make_async_remote_copy(
            src_ref=reduced.at[i, 1 - half_place], dst_ref=from_core.at[i],
            send_sem=core_send.at[i], recv_sem=core_recv.at[i],
            device_id={"crow": c + 1 - 2 * half_place}, device_id_type=MESH,
        )

    def far_copy(i):
        return pltpu.make_async_remote_copy(
            src_ref=summed.at[i, 1 - pair_place], dst_ref=from_far.at[i],
            send_sem=far_send.at[i], recv_sem=far_recv.at[i],
            device_id={"crow": c + 2 - 4 * pair_place}, device_id_type=MESH,
        )

    def scatter(i, part, pivot_rows):
        p0, p1, p2 = thirds(pivot_rows)
        part = part - dot(wide, jnp.concatenate([p0, p1, p0, p1, p2, p0], axis=0))
        for place in range(crow_count):
            reduced[i, place % 2, place // 2] = part[place * share:(place + 1) * share]
        core_copy(i).start()

    def pass_on(i):
        core_copy(i).wait_recv()
        summed[i] = reduced[i, half_place] + from_core[i]
        far_copy(i).start()

    def gather(i):
        far_copy(i).wait_recv()
        return summed[i, pair_place] + from_far[i]

    scatter(slots, gram, gram_pivot)

    for j in order:
        i = slots - 1 - j

        @pl.when(inside[i])
        def _():
            tile_copy(j).wait_recv()
            here = dot(own[i], arrived[i])
            product[...] = here.reshape(product.shape)
            scatter(i, here, product[owner])

    pass_on(slots)
    for j in order:
        @pl.when(inside[slots - 1 - j])
        def _():
            pass_on(slots - 1 - j)

    self_out[...] = gather(slots)
    for j in order:
        i = slots - 1 - j

        @pl.when(inside[i])
        def _():
            coupling_out[:, i * width:(i + 1) * width] = gather(i)

        @pl.when(jnp.logical_not(inside[i]))
        def _():
            coupling_out[:, i * width:(i + 1) * width] = jnp.zeros((share, width), F32)

    @pl.when(has_right)
    def _():
        halo(0).wait_send()
        halo(1).wait_send()

    @pl.when(has_left)
    def _():
        halo(2).wait_send()

    for r in range(1, crow_count):
        pivot_copy(r).wait_send()
    core_copy(slots).wait_send()
    far_copy(slots).wait_send()
    for j in range(slots):
        @pl.when(inside[j])
        def _():
            tile_copy(j).wait_send()
            core_copy(j).wait_send()
            far_copy(j).wait_send()


def hand_over(a, b, c, a_out, b_out, c_out, sem):
    copies = [
        pltpu.make_async_copy(source, target, sem.at[k])
        for k, (source, target) in enumerate(((b, b_out), (a, a_out), (c, c_out)))
    ]
    for copy in copies:
        copy.start()
    for copy in copies:
        copy.wait()


def per_device(deflation, diag_op, upper_op, tile_blocks, pair_counts, pivot_owner):
    crow_count = lax.axis_size("crow")
    sub_count = lax.axis_size("sub")
    offsets = neighbour_offsets(min(16, sub_count // 2))
    blocks, rows = diag_op.shape[1], diag_op.shape[2]
    width = deflation.shape[2]
    slots = pair_counts.shape[1]
    per_slot = tile_blocks.shape[2] // slots
    share = width // crow_count
    others = crow_count - 1
    vmem = pl.BlockSpec(memory_space=pltpu.VMEM)
    smem = pl.BlockSpec(memory_space=pltpu.SMEM)
    hbm = pl.BlockSpec(memory_space=pltpu.HBM)
    dma = pltpu.SemaphoreType.DMA
    results = pl.pallas_call(
        functools.partial(kernel, offsets, sub_count, crow_count),
        out_shape=(
            pltpu.VMEM((share, width), F32),
            pltpu.VMEM((share, slots * width), F32),
            pltpu.VMEM((share, share), F32),
        ),
        in_specs=[hbm, hbm, hbm, smem, smem, smem],
        out_specs=(vmem, vmem, vmem),
        scratch_shapes=[
            pltpu.VMEM((blocks + 2, rows, width), BF16),
            pltpu.VMEM((blocks + 2, width, rows), BF16),
            pltpu.VMEM((blocks, rows, rows), BF16),
            pltpu.VMEM((blocks + 1, rows, rows), BF16),
            pltpu.VMEM((blocks, width, rows), BF16),
            pltpu.VMEM((slots, per_slot * rows, width), BF16),
            pltpu.VMEM((slots, per_slot * rows, width), BF16),
            pltpu.VMEM((slots, width, per_slot * rows), BF16),
            pltpu.VMEM((crow_count, share, width), F32),
            pltpu.VMEM((slots + 1, 2, 2, share, width), F32),
            pltpu.VMEM((slots + 1, 2, share, width), F32),
            pltpu.VMEM((slots + 1, 2, share, width), F32),
            pltpu.VMEM((slots + 1, share, width), F32),
            pltpu.VMEM((crow_count, share, width), F32),
            pltpu.VMEM((crow_count, share, width), F32),
            pltpu.VMEM((share, width), F32),
            dma((3, 2)), dma((3,)), dma((3,)),
            dma((slots,)), dma((slots,)),
            dma((others,)), dma((others,)),
            dma((slots + 1,)), dma((slots + 1,)), dma((slots + 1,)), dma((slots + 1,)),
        ],
        compiler_params=pltpu.CompilerParams(
            collective_id=0, has_side_effects=True, vmem_limit_bytes=VMEM_BYTES
        ),
    )(
        deflation.reshape(blocks, rows, width),
        diag_op.reshape(blocks, rows, rows),
        upper_op.reshape(blocks, rows, rows),
        tile_blocks, pair_counts, pivot_owner,
    )
    return pl.pallas_call(
        hand_over,
        out_shape=tuple(jax.ShapeDtypeStruct(x.shape, F32) for x in results),
        in_specs=[vmem] * 3,
        out_specs=(hbm,) * 3,
        scratch_shapes=[dma((3,))],
        compiler_params=pltpu.CompilerParams(vmem_limit_bytes=2 * 1024 * 1024),
    )(*results)


def solution(mesh):
    placed = (
        P("sub", "crow", None),
        P("sub", "crow", None, None),
        P("sub", "crow", None, None),
        P("sub", "crow", None),
        P("sub", None),
        P("sub"),
    )
    return jax.shard_map(
        per_device,
        mesh=mesh,
        in_specs=placed,
        out_specs=(P(("sub", "crow"), None), P(("sub", "crow"), None), P(("sub", "crow"), None)),
        check_vma=False,
    )
```
